32 devices in a mesh: groups: 2 (over y), sector: 4 (over z), mpo: 4 (over x, core).
Axes of the slice: x: 2, y: 2, z: 4, core: 2. Of those that a mesh axis runs over, the one named last changes fastest.
Arguments:
- wavefunction: float32 [1024, 512], P(('groups', 'sector')), parts along dimension 0
- left_environment: float32 [16, 1024, 128], P('mpo', ('groups', 'sector')), parts along dimension 1, may hold values from -0.125 to 0.125
- right_environment: float32 [16, 1024, 128], P('mpo', ('groups', 'sector')), parts along dimension 1, may hold values from -0.5 to 0.5
- left_sizes: int32 [8], P('groups'), parts along dimension 0, may hold values from 32 to 128, as said below
- right_sizes: int32 [8], P('groups'), parts along dimension 0, may hold values from 32 to 128, as said below
- sector_pairs: int32 [8, 4], P('groups'), parts along dimension 0, may hold values from 0 to 1, as said below
Outputs:
- product: float32 [1024, 512], P(('groups', 'sector')), parts along dimension 0
- ritz_value: float32 [2], P('groups'), parts along dimension 0
The draws below stay inside these ranges and needn't reach their ends.
There are 2 independent parts, one for each index of `groups`. The reference program is written for one: setup_inputs(seed, part) draws one part's arguments, and reference() takes and returns one part's arrays. A program takes and returns all parts, laid end to end along the dimension named above; each array names one. Nothing has to cross between parts.
Inputs may be any that keep to these rules, and one draw needn't show every extreme that they name: `left_sizes`: some left sector has exactly 128 states. `right_sizes`: some right sector has exactly 128 states. `sector_pairs`: every left sector has at least one allowed right sector.
All inputs are finite; a program needn't handle non-finite values.
Results may differ from the reference program's by a relative error of at most 0.0002.
Values sent between devices are 32-bit elements; how exact they have to be, the bound alone decides.
No kernel may reach another device: no remote copies, remote signals or barrier semaphores. Data moves between devices by JAX's collectives and lax.ppermute only.
A program may use at most 64 MiB of HBM per device.

```python
import jax
import jax.numpy as jnp
from jax import lax

W = 16
DL = 128
DR = 128
NSEC = 4
NL = 512
NR = 512


def sector_widths(key, largest):
    step_key, pick_key = jax.random.split(key)
    widths = jax.random.randint(step_key, (NSEC,), largest // 4, largest + 1)
    chosen = jax.random.randint(pick_key, (), 0, NSEC)
    return jnp.where(jnp.arange(NSEC) == chosen, largest, widths).astype(jnp.int32)


def draw_left_sizes(key, part):
    key = jax.random.fold_in(key, 21)
    return sector_widths(key, DL)


def draw_right_sizes(key, part):
    key = jax.random.fold_in(key, 22)
    return sector_widths(key, DR)


def draw_sector_pairs(key, part):
    key = jax.random.fold_in(key, 23)
    coin_key, order_key = jax.random.split(key)
    coin_flips = jax.random.randint(coin_key, (NSEC, NSEC), 0, 2)
    partner_order = jax.random.permutation(order_key, NSEC)
    forced = (partner_order[:, None] == jnp.arange(NSEC)[None, :]).astype(jnp.int32)
    return jnp.maximum(coin_flips, forced).astype(jnp.int32)


def draw_wavefunction(key, part):
    key = jax.random.fold_in(key, 11)
    base_key, row_key, col_key = jax.random.split(key, 3)
    base = jax.random.normal(base_key, (NL, NR), jnp.float32)
    row_scale = jnp.exp(jax.random.uniform(row_key, (NSEC, 1, 1, 1), jnp.float32, -1.0, 1.0))
    col_scale = jnp.exp(jax.random.uniform(col_key, (1, 1, NSEC, 1), jnp.float32, -1.0, 1.0))
    return (base.reshape(NSEC, DL, NSEC, DR) * row_scale * col_scale).reshape(NL, NR)


def level_of(stream_key, extent, pieces, least, high):
    def one(axis_at, parts):
        draws = jax.random.uniform(jax.random.fold_in(jax.random.fold_in(stream_key, 6), axis_at), (parts,), jnp.float32, least / len(pieces), high / len(pieces))
        return jnp.repeat(jnp.exp(draws), extent[axis_at] // parts).reshape((-1,) + (1,) * (len(extent) - axis_at - 1))

    level = one(*pieces[0])
    for cut in pieces[1:]:
        level = level * one(*cut)
    return level


def noise(stream_key, dims, deviation, limit, cuts=(), held_as=jnp.bfloat16):
    entries = jax.random.normal(stream_key, dims, jnp.float32) * deviation
    if len(cuts) > 0:
        entries = level_of(stream_key, dims, cuts, -0.22, 0.18) * entries
    return jnp.clip(entries, min=-limit, max=limit).astype(held_as)


def setup_inputs(seed: int = 0, part: int = 0) -> dict:
    keys = jax.random.split(jax.random.key(seed), 7)
    part_keys = jax.random.split(jax.random.fold_in(keys[6], part), 7)
    return {
        "wavefunction": draw_wavefunction(jax.random.fold_in(jax.random.fold_in(keys[6], part), 71), part),
        "left_environment": noise(part_keys[1], (W, NL, DL), (DL * W) ** -0.5, 0.125, ((0, 4), (1, 4)), jnp.float32),
        "right_environment": noise(part_keys[2], (W, NR, DR), DR ** -0.5, 0.5, ((0, 4), (1, 4)), jnp.float32),
        "left_sizes": draw_left_sizes(jax.random.fold_in(jax.random.fold_in(keys[6], part), 71), part),
        "right_sizes": draw_right_sizes(jax.random.fold_in(jax.random.fold_in(keys[6], part), 71), part),
        "sector_pairs": draw_sector_pairs(jax.random.fold_in(jax.random.fold_in(keys[6], part), 71), part),
    }


EXACT = lax.Precision.HIGHEST
TINY = 1e-06

def sector_valid(left_sizes, right_sizes, sector_pairs):
    row_valid = (jnp.arange(DL)[None, :] < left_sizes[:, None]).astype(jnp.float32)
    col_valid = (jnp.arange(DR)[None, :] < right_sizes[:, None]).astype(jnp.float32)
    pair_valid = sector_pairs.astype(jnp.float32)
    return row_valid[:, :, None, None] * pair_valid[:, None, :, None] * col_valid[None, None, :, :]

def apply_hamiltonian(vector, left_environment, right_environment, valid_mask):
    blocks = vector.reshape(NSEC, DL, NSEC, DR)
    left_blocks = left_environment.reshape(W, NSEC, DL, DL)
    right_blocks = right_environment.reshape(W, NSEC, DR, DR)

    def channel(summed, channel_index):
        halfway = jnp.einsum('aik,akbc->aibc', left_blocks[channel_index], blocks, precision=EXACT)
        summed = summed + jnp.einsum('aibc,bjc->aibj', halfway, right_blocks[channel_index], precision=EXACT)
        return (summed, None)
    summed, unused = lax.scan(channel, jnp.zeros((NSEC, DL, NSEC, DR), jnp.float32), jnp.arange(W))
    return (summed * valid_mask).reshape(NL, NR)

def reference(wavefunction, left_environment, right_environment, left_sizes, right_sizes, sector_pairs):
    valid_mask = sector_valid(left_sizes, right_sizes, sector_pairs)
    vector = (wavefunction.reshape(NSEC, DL, NSEC, DR) * valid_mask).reshape(NL, NR)
    first_image = apply_hamiltonian(vector, left_environment, right_environment, valid_mask)
    cross_term = jnp.sum(vector * first_image)
    self_term = jnp.sum(vector * vector)
    ritz_value = cross_term / (self_term + TINY)
    residual = first_image - ritz_value * vector
    square_total = jnp.sum(residual * residual)
    following = residual / jnp.sqrt(square_total / (NL * NR) + TINY)
    product = apply_hamiltonian(following, left_environment, right_environment, valid_mask)
    return (product, jnp.reshape(ritz_value, (1,)))
```

```python
import functools

import jax
import jax.numpy as jnp
from jax import lax
from jax.experimental import pallas as pl
from jax.experimental.pallas import tpu as pltpu
from jax.sharding import PartitionSpec as P

EXACT = lax.Precision.HIGHEST
TINY = 1e-06
VMEM = pl.BlockSpec(memory_space=pltpu.VMEM)
SMEM = pl.BlockSpec(memory_space=pltpu.SMEM)
F32 = jnp.float32


def dot_nn(a, b):
    return lax.dot_general(
        a, b, (((1,), (0,)), ((), ())), precision=EXACT, preferred_element_type=F32
    )


def dot_nt(a, b):
    return lax.dot_general(
        a, b, (((1,), (1,)), ((), ())), precision=EXACT, preferred_element_type=F32
    )


def block_valid(left_sizes, right_sizes, pairs, a, b, rows, cols):
    row = lax.broadcasted_iota(jnp.int32, (rows, cols), 0) < left_sizes[a]
    col = lax.broadcasted_iota(jnp.int32, (rows, cols), 1) < right_sizes[b]
    return (row & col).astype(F32) * pairs[a, b].astype(F32)


def call(body, outs, n_small, n_big, **kw):
    return pl.pallas_call(
        body,
        out_shape=outs,
        in_specs=[SMEM] * n_small + [VMEM] * n_big,
        out_specs=[VMEM] * len(outs),
        compiler_params=pltpu.CompilerParams(vmem_limit_bytes=32 * 1024 * 1024),
        **kw,
    )


def slot_column(slot, sector):
    low = sector < 2
    if slot == 0:
        return sector
    if slot == 1:
        return sector ^ 1
    if slot == 2:
        return jnp.where(low, 2, 1)
    return jnp.where(low, 3, 0)


def half_body(left_sizes, right_sizes, pairs, wave, left, vector, halfway):
    sector = lax.axis_index("sector")
    channels, rows, _ = left.shape
    sectors, _, inner = halfway.shape
    cols = inner // channels
    for b in range(sectors):
        at = slice(b * cols, (b + 1) * cols)
        vector[:, at] = wave[:, at] * block_valid(
            left_sizes, right_sizes, pairs, sector, b, rows, cols
        )
    for w in range(channels):
        part = dot_nn(left[w], vector[...])
        for b in range(sectors):
            halfway[b, :, w * cols : (w + 1) * cols] = part[:, b * cols : (b + 1) * cols]


def pick(refs, w, sector):
    if len(refs) == 1:
        return refs[0][w]
    middle = (sector == 1) | (sector == 2)
    return jnp.where(middle, refs[0][w], refs[1][w])


def group(refs, ways):
    out, k = [], 0
    for n in ways:
        out.append(refs[k : k + n])
        k += n
    return out


def first_body(slots, ways, halfway, *refs):
    out = refs[-1]
    sector = lax.axis_index("sector")
    rights = group(refs[:-1], ways)
    for k, slot in enumerate(slots):
        b = slot_column(slot, sector)
        channels, cols, _ = rights[k][0].shape
        total = None
        for w in range(channels):
            part = dot_nt(
                halfway[b, :, w * cols : (w + 1) * cols], pick(rights[k], w, sector)
            )
            total = part if total is None else total + part
        out[k] = total


def second_body(slots, ways, left_sizes, right_sizes, pairs, own, other, vector, left, *refs):
    image, partial, sums = refs[-3:]
    sector = lax.axis_index("sector")
    rights = group(refs[:-3], ways)
    channels, rows, _ = left.shape
    cross = jnp.zeros((1, 1), F32)
    square = jnp.zeros((1, 1), F32)
    vectors = []
    for k, slot in enumerate(slots):
        b = slot_column(slot, sector)
        cols = own.shape[2]
        valid = block_valid(left_sizes, right_sizes, pairs, sector, b, rows, cols)
        here = (own[k] + other[k]) * valid
        image[k] = here
        v = vector[:, pl.ds(pl.multiple_of(b * cols, cols), cols)]
        vectors.append(v)
        cross += jnp.sum(v * here, keepdims=True)
        square += jnp.sum(v * v, keepdims=True)
        total = None
        for w in range(channels):
            part = dot_nt(dot_nn(left[w], here), pick(rights[k], w, sector))
            total = part if total is None else total + part
        partial[k] = total
    ratio = jnp.where(square > 0, cross / jnp.where(square > 0, square, 1.0), 0.0)
    rest = jnp.zeros((1, 1), F32)
    for k in range(len(slots)):
        away = image[k] - ratio * vectors[k]
        rest += jnp.sum(away * away, keepdims=True)
    row = lax.broadcasted_iota(jnp.int32, sums.shape, 0)
    sums[...] = jnp.where(row == 0, cross, jnp.where(row == 1, square, rest))


def last_body(slots_a, slots_b, cells, left_sizes, right_sizes, pairs, *refs):
    sums = refs[:8]
    own_a, other_a, image_a, own_b, other_b, image_b, product, ritz = refs[8:]
    sector = lax.axis_index("sector")


    def added(terms):
        while len(terms) > 1:
            terms = [x + y for x, y in zip(terms[::2], terms[1::2])]
        return terms[0]

    value = added([s[0:1, :] for s in sums]) / (added([s[1:2, :] for s in sums]) + TINY)
    rests = []
    for s in sums:
        c = s[1:2, :]
        ratio = jnp.where(c > 0, s[0:1, :] / jnp.where(c > 0, c, 1.0), 0.0)
        rests.append(s[2:3, :] + (ratio - value) * (ratio - value) * c)
    rest = added(rests)
    scale = 1.0 / jnp.sqrt(rest / cells + TINY)
    ritz[...] = jnp.broadcast_to(value, ritz.shape)
    for slots, own, other, image in (
        (slots_a, own_a, other_a, image_a),
        (slots_b, own_b, other_b, image_b),
    ):
        for k, slot in enumerate(slots):
            b = slot_column(slot, sector)
            _, rows, cols = own.shape
            valid = block_valid(left_sizes, right_sizes, pairs, sector, b, rows, cols)
            out = ((own[k] + other[k]) * valid - value * image[k]) * scale
            product[:, pl.ds(pl.multiple_of(b * cols, cols), cols)] = out


def line_device(wave, left, right, left_sizes, right_sizes, pairs):
    channels, rows, _ = left.shape
    cols = right.shape[2]
    sectors = 4
    cells = float(sectors * rows * sectors * cols)
    small = (left_sizes, right_sizes, pairs)

    def outer(x):
        return lax.ppermute(x, "sector", [(0, 1), (1, 0), (2, 3), (3, 2)])

    def inner(x):
        return lax.ppermute(x, "sector", [(1, 2), (2, 1), (0, 0), (3, 3)])

    def core(x):
        return lax.ppermute(x, "mpo", [(0, 1), (1, 0), (2, 3), (3, 2)])

    def across(x):
        return lax.ppermute(x, "mpo", [(0, 2), (1, 3), (2, 0), (3, 1)])

    def shape(*dims):
        return jax.ShapeDtypeStruct(dims, F32)

    out1 = outer(right)
    in1 = inner(right)
    vector, halfway = call(
        half_body, [shape(rows, sectors * cols), shape(sectors, rows, channels * cols)], 3, 2
    )(*small, wave, left)
    in2 = inner(out1)
    out2 = outer(in1)
    out3 = outer(in2)

    groups = (
        ((0, 1, 2), (1, 1, 2), (right, out1, in1, out2)),
        ((3,), (2,), (in2, out3)),
    )
    images, totals, sums = [], [], []
    for slots, ways, rights in groups:
        n = len(slots)
        (partial,) = call(
            functools.partial(first_body, slots, ways), [shape(n, rows, cols)], 0, 1 + len(rights)
        )(halfway, *rights)
        both = partial + core(partial)
        image, partial, total = call(
            functools.partial(second_body, slots, ways),
            [shape(n, rows, cols), shape(n, rows, cols), shape(8, cols)],
            3,
            4 + len(rights),
        )(*small, both, across(both), vector, left, *rights)
        both = partial + core(partial)
        images.append(image)
        totals.append((both, across(both)))
        sums.append(total)

    mine = jnp.concatenate(sums)
    near = lax.ppermute(mine, "sector", [(0, 1), (1, 0), (2, 3), (3, 2)])
    far = lax.ppermute(mine, "sector", [(0, 2), (2, 0), (1, 3), (3, 1)])
    cross = lax.ppermute(mine, "sector", [(0, 3), (3, 0), (1, 2), (2, 1)])
    everyone = [s[i : i + 8] for s in (mine, near, far, cross) for i in (0, 8)]
    product, ritz = call(
        functools.partial(last_body, groups[0][0], groups[1][0], cells),
        [shape(rows, sectors * cols), shape(8, cols)],
        3,
        14,
    )(*small, *everyone, *totals[0], images[0], *totals[1], images[1])
    return product, ritz[0, :1]


def wide_device(wave, left, right, left_sizes, right_sizes, pairs):
    sector = lax.axis_index("sector")
    sectors = lax.axis_size("sector")
    channels, rows, _ = left.shape
    cols = right.shape[2]
    cells = float(sectors * rows * sectors * cols)
    own = lax.dynamic_index_in_dim(pairs, sector, 0, keepdims=False).astype(F32)
    size = lax.dynamic_index_in_dim(left_sizes, sector, 0, keepdims=False)
    row = (jnp.arange(rows) < size).astype(F32)
    col = (jnp.arange(cols)[None, :] < right_sizes[:, None]).astype(F32) * own[:, None]
    valid = row[:, None] * col.reshape(1, -1)
    vector = wave * valid
    rights = lax.all_gather(right, "sector", axis=1)

    def image_of(v):
        half = jnp.einsum("wik,kbc->wibc", left, v.reshape(rows, sectors, cols), precision=EXACT)
        out = jnp.einsum("wibc,wbjc->ibj", half, rights, precision=EXACT)
        return lax.psum(out.reshape(rows, sectors * cols), "mpo") * valid

    first = image_of(vector)
    cross, square = lax.psum((jnp.sum(vector * first), jnp.sum(vector * vector)), "sector")
    value = cross / (square + TINY)
    residual = first - value * vector
    rest = lax.psum(jnp.sum(residual * residual), "sector")
    product = image_of(residual / jnp.sqrt(rest / cells + TINY))
    return product, jnp.reshape(value, (1,))


def solution(mesh):
    line = mesh.shape["sector"] == 4 and mesh.shape["mpo"] == 4
    return jax.shard_map(
        line_device if line else wide_device,
        mesh=mesh,
        in_specs=(
            P(("groups", "sector"), None),
            P("mpo", ("groups", "sector"), None),
            P("mpo", ("groups", "sector"), None),
            P("groups"),
            P("groups"),
            P("groups", None),
        ),
        out_specs=(P(("groups", "sector"), None), P("groups")),
        check_vma=False,
    )
```

```python
import functools

import jax
import jax.numpy as jnp
from jax import lax
from jax.experimental import pallas as pl
from jax.experimental.pallas import tpu as pltpu
from jax.sharding import PartitionSpec as P

EXACT = lax.Precision.HIGHEST
TINY = 1e-06
VMEM = pl.BlockSpec(memory_space=pltpu.VMEM)
SMEM = pl.BlockSpec(memory_space=pltpu.SMEM)
F32 = jnp.float32
BF16 = jnp.bfloat16


def split(x):
    high = x.astype(BF16)
    return high, (x - high.astype(F32)).astype(BF16)


def left_terms(x, axis):
    high, low = split(x)
    return jnp.concatenate([high, high, low], axis=axis)


def right_terms(x, axis):
    high, low = split(x)
    return jnp.concatenate([high, low, high], axis=axis)


def dot_nn(a, b):
    return lax.dot_general(a, b, (((1,), (0,)), ((), ())), preferred_element_type=F32)


def dot_nt(a, b):
    return lax.dot_general(a, b, (((1,), (1,)), ((), ())), preferred_element_type=F32)


def block_valid(left_sizes, right_sizes, pairs, a, b, rows, cols):
    row = lax.broadcasted_iota(jnp.int32, (rows, cols), 0) < left_sizes[a]
    col = lax.broadcasted_iota(jnp.int32, (rows, cols), 1) < right_sizes[b]
    return (row & col).astype(F32) * pairs[a, b].astype(F32)


def call(body, outs, n_small, n_big, **kw):
    return pl.pallas_call(
        body,
        out_shape=outs,
        in_specs=[SMEM] * n_small + [VMEM] * n_big,
        out_specs=[VMEM] * len(outs),
        compiler_params=pltpu.CompilerParams(vmem_limit_bytes=32 * 1024 * 1024),
        **kw,
    )


def slot_column(slot, sector):
    return sector ^ (0, 1, 3, 2)[slot]


def columns(b, width):
    return pl.ds(pl.multiple_of(b * width, width), width)


def channel_row(blocks):
    return jnp.concatenate([blocks[w] for w in range(blocks.shape[0])], axis=1)


def half_body(left_sizes, right_sizes, pairs, wave, left, vector, halfway, factors):
    sector = lax.axis_index("sector")
    channels, rows, _ = left.shape
    sectors, _, inner = halfway.shape
    cols = inner // channels
    factors[...] = left_terms(left[...].reshape(channels * rows, rows), 1)
    for b in range(sectors):
        at = slice(b * cols, (b + 1) * cols)
        here = wave[:, at] * block_valid(left_sizes, right_sizes, pairs, sector, b, rows, cols)
        vector[:, at] = here
        part = dot_nn(factors[...], right_terms(here, 0))
        for w in range(channels):
            halfway[b, :, w * cols : (w + 1) * cols] = part[w * rows : (w + 1) * rows]


def first_body(slots, halfway, *refs):
    out = refs[-1]
    sector = lax.axis_index("sector")
    for k, slot in enumerate(slots):
        out[k] = dot_nt(
            left_terms(halfway[slot_column(slot, sector)], 1),
            right_terms(channel_row(refs[k]), 1),
        )


def second_body(slots, left_sizes, right_sizes, pairs, own, other, vector, factors, *refs):
    n = len(slots)
    image, partial, sums = refs[-3:]
    sector = lax.axis_index("sector")
    _, rows, cols = own.shape
    channels = factors.shape[0] // rows
    cross = jnp.zeros((1, cols), F32)
    square = jnp.zeros((1, cols), F32)
    vectors = []
    for k, slot in enumerate(slots):
        b = slot_column(slot, sector)
        valid = block_valid(left_sizes, right_sizes, pairs, sector, b, rows, cols)
        here = (own[k] + other[k]) * valid
        image[k] = here
        half = dot_nn(factors[...], right_terms(here, 0))
        half = channel_row(half.reshape(channels, rows, cols))
        partial[k] = dot_nt(left_terms(half, 1), right_terms(channel_row(refs[k]), 1))
        v = vector[:, columns(b, cols)]
        vectors.append(v)
        cross += jnp.sum(v * here, axis=0, keepdims=True)
        square += jnp.sum(v * v, axis=0, keepdims=True)
    ratio = jnp.where(square > 0, cross / jnp.where(square > 0, square, 1.0), 0.0)
    rest = jnp.zeros((1, cols), F32)
    for k in range(n):
        away = image[k] - ratio * vectors[k]
        rest += jnp.sum(away * away, axis=0, keepdims=True)
    if len(refs) > n + 3:
        sums[...] = refs[n][...]
        at = 3
    else:
        sums[...] = jnp.zeros_like(sums)
        at = 0
    sums[at : at + 1, :] = cross
    sums[at + 1 : at + 2, :] = square
    sums[at + 2 : at + 3, :] = rest


def last_body(groups, cells, left_sizes, right_sizes, pairs, *refs):
    mine, near, far, cross = refs[:4]
    product, ritz = refs[-2:]
    sector = lax.axis_index("sector")

    def everyone(read):
        lanes = (read(mine) + read(near)) + (read(far) + read(cross))
        return jnp.sum(lanes)

    def both(row):
        return lambda s: s[row : row + 1, :] + s[row + 3 : row + 4, :]

    value = everyone(both(0)) / (everyone(both(1)) + TINY)

    def rest_of(s):
        total = s[2:3, :] + s[5:6, :]
        for row in (0, 3):
            c = s[row + 1 : row + 2, :]
            ratio = jnp.where(c > 0, s[row : row + 1, :] / jnp.where(c > 0, c, 1.0), 0.0)
            total += (ratio - value) * (ratio - value) * c
        return total

    scale = 1.0 / jnp.sqrt(everyone(rest_of) / cells + TINY)
    ritz[0] = value
    at = 4
    for slots in groups:
        own, other, image = refs[at : at + 3]
        at += 3
        for k, slot in enumerate(slots):
            b = slot_column(slot, sector)
            _, rows, cols = own.shape
            valid = block_valid(left_sizes, right_sizes, pairs, sector, b, rows, cols)
            product[:, columns(b, cols)] = (
                (own[k] + other[k]) * valid - value * image[k]
            ) * scale


def line_device(wave, left, right, left_sizes, right_sizes, pairs):
    channels, rows, _ = left.shape
    cols = right.shape[2]
    sectors = 4
    cells = float(sectors * rows * sectors * cols)
    small = (left_sizes, right_sizes, pairs)

    def near(x):
        return lax.ppermute(x, "sector", [(0, 1), (1, 0), (2, 3), (3, 2)])

    def far(x):
        return lax.ppermute(x, "sector", [(0, 2), (2, 0), (1, 3), (3, 1)])

    def mirror(x):
        return lax.ppermute(x, "sector", [(0, 3), (3, 0), (1, 2), (2, 1)])

    def core(x):
        return lax.ppermute(x, "mpo", [(0, 1), (1, 0), (2, 3), (3, 2)])

    def across(x):
        return lax.ppermute(x, "mpo", [(0, 2), (1, 3), (2, 0), (3, 1)])

    def shape(*dims, of=F32):
        return jax.ShapeDtypeStruct(dims, of)

    right_near = near(right)
    right_mirror = mirror(right)
    right_far = near(right_mirror)
    vector, halfway, factors = call(
        half_body,
        [
            shape(rows, sectors * cols),
            shape(sectors, rows, channels * cols),
            shape(channels * rows, 3 * rows, of=BF16),
        ],
        3,
        2,
    )(*small, wave, left)

    groups = ((0, 1), (2, 3))
    rights = ((right, right_near), (right_mirror, right_far))
    parts = []
    sums = ()
    for slots, envs in zip(groups, rights):
        n = len(slots)
        (partial,) = call(
            functools.partial(first_body, slots), [shape(n, rows, cols)], 0, 1 + n
        )(halfway, *envs)
        both = partial + core(partial)
        image, partial, total = call(
            functools.partial(second_body, slots),
            [shape(n, rows, cols), shape(n, rows, cols), shape(8, cols)],
            3,
            4 + n + len(sums),
        )(*small, both, across(both), vector, factors, *envs, *sums)
        sums = (total,)
        both = partial + core(partial)
        parts += [both, across(both), image]

    (mine,) = sums
    product, ritz = pl.pallas_call(
        functools.partial(last_body, groups, cells),
        out_shape=[shape(rows, sectors * cols), shape(1)],
        in_specs=[SMEM] * 3 + [VMEM] * 10,
        out_specs=[VMEM, SMEM],
    )(*small, mine, near(mine), far(mine), mirror(mine), *parts)
    return product, ritz


def wide_device(wave, left, right, left_sizes, right_sizes, pairs):
    sector = lax.axis_index("sector")
    sectors = lax.axis_size("sector")
    channels, rows, _ = left.shape
    cols = right.shape[2]
    cells = float(sectors * rows * sectors * cols)
    own = lax.dynamic_index_in_dim(pairs, sector, 0, keepdims=False).astype(F32)
    size = lax.dynamic_index_in_dim(left_sizes, sector, 0, keepdims=False)
    row = (jnp.arange(rows) < size).astype(F32)
    col = (jnp.arange(cols)[None, :] < right_sizes[:, None]).astype(F32) * own[:, None]
    valid = row[:, None] * col.reshape(1, -1)
    vector = wave * valid
    rights = lax.all_gather(right, "sector", axis=1)

    def image_of(v):
        half = jnp.einsum("wik,kbc->wibc", left, v.reshape(rows, sectors, cols), precision=EXACT)
        out = jnp.einsum("wibc,wbjc->ibj", half, rights, precision=EXACT)
        return lax.psum(out.reshape(rows, sectors * cols), "mpo") * valid

    first = image_of(vector)
    cross, square = lax.psum((jnp.sum(vector * first), jnp.sum(vector * vector)), "sector")
    value = cross / (square + TINY)
    residual = first - value * vector
    rest = lax.psum(jnp.sum(residual * residual), "sector")
    product = image_of(residual / jnp.sqrt(rest / cells + TINY))
    return product, jnp.reshape(value, (1,))


def solution(mesh):
    line = mesh.shape["sector"] == 4 and mesh.shape["mpo"] == 4
    return jax.shard_map(
        line_device if line else wide_device,
        mesh=mesh,
        in_specs=(
            P(("groups", "sector"), None),
            P("mpo", ("groups", "sector"), None),
            P("mpo", ("groups", "sector"), None),
            P("groups"),
            P("groups"),
            P("groups", None),
        ),
        out_specs=(P(("groups", "sector"), None), P("groups")),
        check_vma=False,
    )
```

```python
import functools

import jax
import jax.numpy as jnp
from jax import lax
from jax.experimental import pallas as pl
from jax.experimental.pallas import tpu as pltpu
from jax.sharding import PartitionSpec as P

EXACT = lax.Precision.HIGHEST
TINY = 1e-06
PARAMS = pltpu.CompilerParams(vmem_limit_bytes=32 * 1024 * 1024)
VMEM = pl.BlockSpec(memory_space=pltpu.VMEM)
SMEM = pl.BlockSpec(memory_space=pltpu.SMEM)
F32 = jnp.float32
BF16 = jnp.bfloat16

EARLY, LATE = (0, 1, 2), (3,)


def split(x):
    high = x.astype(BF16)
    return high, (x - high.astype(F32)).astype(BF16)


def left_terms(x):
    high, low = split(x)
    return jnp.concatenate([high, high, low], axis=1)


def right_terms(x):
    high, low = split(x)
    return jnp.concatenate([high, low, high], axis=0)


def times(a, b):
    return lax.dot_general(a, b, (((1,), (0,)), ((), ())), preferred_element_type=F32)


def times_turned(a, b):
    m, n = a.shape[0], b.shape[0]
    both = lax.dot_general(
        jnp.concatenate(split(a), axis=0),
        jnp.concatenate(split(b), axis=0),
        (((1,), (1,)), ((), ())),
        preferred_element_type=F32,
    )
    return (both[m:, n:] + (both[m:, :n] + both[:m, n:])) + both[:m, :n]


def block_valid(left_sizes, right_sizes, pairs, a, b, rows, cols):
    row = lax.broadcasted_iota(jnp.int32, (rows, cols), 0) < left_sizes[a]
    col = lax.broadcasted_iota(jnp.int32, (rows, cols), 1) < right_sizes[b]
    return (row & col).astype(F32) * pairs[a, b].astype(F32)


def call(body, outs, n_small, n_big):
    return pl.pallas_call(
        body,
        out_shape=outs,
        in_specs=[SMEM] * n_small + [VMEM] * n_big,
        out_specs=[VMEM] * len(outs),
        compiler_params=PARAMS,
    )


def slot_column(slot, sector):
    return sector ^ (0, 1, 3, 2)[slot]


def columns(b, width):
    return pl.ds(pl.multiple_of(b * width, width), width)


def channel_row(blocks):
    return jnp.concatenate([blocks[w] for w in range(blocks.shape[0])], axis=1)


def half_body(left_sizes, right_sizes, pairs, wave, left, vector, halfway, factors, valid):
    sector = lax.axis_index("sector")
    channels, rows, _ = left.shape
    slots, _, inner = halfway.shape
    cols = inner // channels
    factors[...] = left_terms(left[...].reshape(channels * rows, rows))
    for k in range(slots):
        b = slot_column(k, sector)
        valid[k] = block_valid(left_sizes, right_sizes, pairs, sector, b, rows, cols)
        vector[k] = wave[:, columns(b, cols)] * valid[k]
    part = times(factors[...], right_terms(channel_row(vector)))
    for k in range(slots):
        for w in range(channels):
            halfway[k, :, w * cols : (w + 1) * cols] = part[
                w * rows : (w + 1) * rows, k * cols : (k + 1) * cols
            ]


def first_body(slots, halfway, *refs):
    out = refs[-1]
    for k, slot in enumerate(slots):
        out[k] = times_turned(halfway[slot], channel_row(refs[k]))


def second_images(slots, own, other, valid, factors, rights, image):
    _, rows, cols = own.shape
    channels = factors.shape[0] // rows
    for k, slot in enumerate(slots):
        image[k] = (own[k] + other[k]) * valid[slot]
    half = times(factors[...], right_terms(channel_row(image)))
    partials = []
    for k in range(len(slots)):
        here = half[:, k * cols : (k + 1) * cols].reshape(channels, rows, cols)
        partials.append(times_turned(channel_row(here), channel_row(rights[k])))
    return partials


def write_sums(slots, vector, image, sums, at):
    cols = vector.shape[2]
    cross = jnp.zeros((1, cols), F32)
    square = jnp.zeros((1, cols), F32)
    for k, slot in enumerate(slots):
        v = vector[slot]
        cross += jnp.sum(v * image[k], axis=0, keepdims=True)
        square += jnp.sum(v * v, axis=0, keepdims=True)
    ratio = jnp.where(square > 0, cross / jnp.where(square > 0, square, 1.0), 0.0)
    rest = jnp.zeros((1, cols), F32)
    for k, slot in enumerate(slots):
        away = image[k] - ratio * vector[slot]
        rest += jnp.sum(away * away, axis=0, keepdims=True)
    sums[at : at + 1, :] = cross
    sums[at + 1 : at + 2, :] = square
    sums[at + 2 : at + 3, :] = rest


def early_body(slots, own, other, valid, factors, vector, *refs):
    image, partial, sums = refs[-3:]
    parts = second_images(slots, own, other, valid, factors, refs[:-3], image)
    for k, part in enumerate(parts):
        partial[k] = part
    sums[...] = jnp.zeros_like(sums)
    write_sums(slots, vector, image, sums, 0)


def late_body(early, slots, own, other, valid, factors, vector, sums_before, before, *refs):
    image, keep, send, sums = refs[-4:]
    me = lax.axis_index("mpo") % 2
    parts = second_images(slots, own, other, valid, factors, refs[:-4], image)
    everything = {slot: before[k] for k, slot in enumerate(early)}
    everything.update(zip(slots, parts))
    for half in (0, 1):

        @pl.when(me == half)
        def _():
            for k in (0, 1):
                keep[k] = everything[2 * half + k]
                send[k] = everything[2 * (1 - half) + k]

    sums[...] = sums_before[...]
    write_sums(slots, vector, image, sums, 3)


def last_body(groups, cells, valid, near, far, *refs):
    product, ritz = refs[-2:]
    sector = lax.axis_index("sector")

    def everyone(read):
        lanes = (read(near, 0) + read(near, 16)) + (read(far, 0) + read(far, 16))
        return jnp.sum(lanes)

    def every_group(row):
        return lambda s, at: sum(
            s[at + row + 3 * g : at + row + 3 * g + 1, :] for g in range(len(groups))
        )

    value = everyone(every_group(0)) / (everyone(every_group(1)) + TINY)

    def rest_of(s, at):
        total = every_group(2)(s, at)
        for row in range(at, at + 3 * len(groups), 3):
            c = s[row + 1 : row + 2, :]
            ratio = jnp.where(c > 0, s[row : row + 1, :] / jnp.where(c > 0, c, 1.0), 0.0)
            total += (ratio - value) * (ratio - value) * c
        return total

    scale = 1.0 / jnp.sqrt(everyone(rest_of) / cells + TINY)
    ritz[0] = value
    total, others = refs[:2]
    me = lax.axis_index("mpo") % 2
    cols = total.shape[2]
    for slots, image in zip(groups, refs[2:-2]):
        for k, slot in enumerate(slots):
            b = slot_column(slot, sector)
            second = jnp.where(me == slot // 2, total[slot % 2], others[slot % 2])
            product[:, columns(b, cols)] = (second * valid[slot] - value * image[k]) * scale


def line_device(wave, left, right, left_sizes, right_sizes, pairs):
    channels, rows, _ = left.shape
    cols = right.shape[2]
    sectors = 4
    cells = float(sectors * rows * sectors * cols)

    def near(x):
        return lax.ppermute(x, "sector", [(0, 1), (1, 0), (2, 3), (3, 2)])

    def far(x):
        return lax.ppermute(x, "sector", [(0, 2), (2, 0), (1, 3), (3, 1)])

    def mirror(x):
        return lax.ppermute(x, "sector", [(0, 3), (3, 0), (1, 2), (2, 1)])

    def core(x):
        return lax.ppermute(x, "mpo", [(0, 1), (1, 0), (2, 3), (3, 2)])

    def across(x):
        return lax.ppermute(x, "mpo", [(0, 2), (1, 3), (2, 0), (3, 1)])

    def shape(*dims, of=F32):
        return jax.ShapeDtypeStruct(dims, of)

    def after(x, *others):
        return lax.optimization_barrier((x, *others))[0]

    right_near = near(right)
    right_mirror = mirror(right)
    vector, halfway, factors, valid = call(
        half_body,
        [
            shape(sectors, rows, cols),
            shape(sectors, rows, channels * cols),
            shape(channels * rows, 3 * rows, of=BF16),
            shape(sectors, rows, cols),
        ],
        3,
        2,
    )(left_sizes, right_sizes, pairs, wave, left)
    right_far = near(after(right_mirror, halfway))

    def partials(slots, halfway, *rights):
        return call(
            functools.partial(first_body, slots), [shape(len(slots), rows, cols)], 0, 1 + len(slots)
        )(halfway, *rights)[0]

    def chip_sum(x):
        return x + core(x)

    one = chip_sum(after(partials((0,), halfway, right), right_mirror))
    two = chip_sum(partials((1, 2), after(halfway, one), right_near, right_mirror))
    three = chip_sum(partials((3,), after(halfway, two), right_far))
    image_early, second_early, sums = call(
        functools.partial(early_body, EARLY),
        [shape(3, rows, cols), shape(3, rows, cols), shape(16, cols)],
        0,
        8,
    )(
        jnp.concatenate([one, two]),
        jnp.concatenate([across(one), across(two)]),
        valid,
        factors,
        vector,
        right,
        right_near,
        right_mirror,
    )
    image_late, keep, send, sums = call(
        functools.partial(late_body, EARLY, LATE),
        [shape(1, rows, cols), shape(2, rows, cols), shape(2, rows, cols), shape(16, cols)],
        0,
        8,
    )(three, across(three), valid, factors, vector, sums, second_early, right_far)

    mine = keep + core(send)
    sums_near = jnp.concatenate([sums, near(sums)])
    sums_far = far(sums_near)
    total = after(mine + across(mine), sums_far)
    others = core(total)
    product, ritz = pl.pallas_call(
        functools.partial(last_body, (EARLY, LATE), cells),
        out_shape=[shape(rows, sectors * cols), shape(1)],
        in_specs=[VMEM] * 7,
        out_specs=[VMEM, SMEM],
        compiler_params=PARAMS,
    )(valid, sums_near, sums_far, total, others, image_early, image_late)
    return product, ritz


def wide_device(wave, left, right, left_sizes, right_sizes, pairs):
    sector = lax.axis_index("sector")
    sectors = lax.axis_size("sector")
    channels, rows, _ = left.shape
    cols = right.shape[2]
    cells = float(sectors * rows * sectors * cols)
    own = lax.dynamic_index_in_dim(pairs, sector, 0, keepdims=False).astype(F32)
    size = lax.dynamic_index_in_dim(left_sizes, sector, 0, keepdims=False)
    row = (jnp.arange(rows) < size).astype(F32)
    col = (jnp.arange(cols)[None, :] < right_sizes[:, None]).astype(F32) * own[:, None]
    valid = row[:, None] * col.reshape(1, -1)
    vector = wave * valid
    rights = lax.all_gather(right, "sector", axis=1)

    def image_of(v):
        half = jnp.einsum("wik,kbc->wibc", left, v.reshape(rows, sectors, cols), precision=EXACT)
        out = jnp.einsum("wibc,wbjc->ibj", half, rights, precision=EXACT)
        return lax.psum(out.reshape(rows, sectors * cols), "mpo") * valid

    first = image_of(vector)
    cross, square = lax.psum((jnp.sum(vector * first), jnp.sum(vector * vector)), "sector")
    value = cross / (square + TINY)
    residual = first - value * vector
    rest = lax.psum(jnp.sum(residual * residual), "sector")
    product = image_of(residual / jnp.sqrt(rest / cells + TINY))
    return product, jnp.reshape(value, (1,))


def solution(mesh):
    line = mesh.shape["sector"] == 4 and mesh.shape["mpo"] == 4
    return jax.shard_map(
        line_device if line else wide_device,
        mesh=mesh,
        in_specs=(
            P(("groups", "sector"), None),
            P("mpo", ("groups", "sector"), None),
            P("mpo", ("groups", "sector"), None),
            P("groups"),
            P("groups"),
            P("groups", None),
        ),
        out_specs=(P(("groups", "sector"), None), P("groups")),
        check_vma=False,
    )
```

```python
import functools

import jax
import jax.numpy as jnp
from jax import lax
from jax.experimental import pallas as pl
from jax.experimental.pallas import tpu as pltpu
from jax.sharding import PartitionSpec as P

EXACT = lax.Precision.HIGHEST
TINY = 1e-06
PARAMS = pltpu.CompilerParams(vmem_limit_bytes=32 * 1024 * 1024)
VMEM = pl.BlockSpec(memory_space=pltpu.VMEM)
SMEM = pl.BlockSpec(memory_space=pltpu.SMEM)
F32 = jnp.float32
BF16 = jnp.bfloat16

EARLY, LATE = (0, 1, 2), (3,)


def split(x):
    high = x.astype(BF16)
    return high, (x - high.astype(F32)).astype(BF16)


def left_terms(x):
    high, low = split(x)
    return jnp.concatenate([high, high, low], axis=1)


def right_terms(x):
    high, low = split(x)
    return jnp.concatenate([high, low, high], axis=0)


def times(a, b):
    return lax.dot_general(a, b, (((1,), (0,)), ((), ())), preferred_element_type=F32)


def times_turned(a, b):
    m, n = a.shape[0], b.shape[0]
    both = lax.dot_general(
        jnp.concatenate(split(a), axis=0),
        jnp.concatenate(split(b), axis=0),
        (((1,), (1,)), ((), ())),
        preferred_element_type=F32,
    )
    return (both[m:, n:] + (both[m:, :n] + both[:m, n:])) + both[:m, :n]


def block_valid(left_sizes, right_sizes, pairs, a, b, rows, cols):
    row = lax.broadcasted_iota(jnp.int32, (rows, cols), 0) < left_sizes[a]
    col = lax.broadcasted_iota(jnp.int32, (rows, cols), 1) < right_sizes[b]
    return (row & col).astype(F32) * pairs[a, b].astype(F32)


def call(body, outs, n_small, n_big, flops=None):
    cost = None
    if flops is not None:
        cost = pl.CostEstimate(flops=flops, bytes_accessed=flops // 100, transcendentals=0)
    return pl.pallas_call(
        body,
        out_shape=outs,
        in_specs=[SMEM] * n_small + [VMEM] * n_big,
        out_specs=[VMEM] * len(outs),
        compiler_params=PARAMS,
        cost_estimate=cost,
    )


def slot_column(slot, sector):
    return sector ^ (0, 1, 3, 2)[slot]


def columns(b, width):
    return pl.ds(pl.multiple_of(b * width, width), width)


def channel_row(blocks):
    return jnp.concatenate([blocks[w] for w in range(blocks.shape[0])], axis=1)


def half_body(left_sizes, right_sizes, pairs, wave, left, vector, halfway, factors, valid):
    sector = lax.axis_index("sector")
    channels, rows, _ = left.shape
    slots, _, inner = halfway.shape
    cols = inner // channels
    factors[...] = left_terms(left[...].reshape(channels * rows, rows))
    for k in range(slots):
        b = slot_column(k, sector)
        valid[k] = block_valid(left_sizes, right_sizes, pairs, sector, b, rows, cols)
        vector[k] = wave[:, columns(b, cols)] * valid[k]
    part = times(factors[...], right_terms(channel_row(vector)))
    for k in range(slots):
        for w in range(channels):
            halfway[k, :, w * cols : (w + 1) * cols] = part[
                w * rows : (w + 1) * rows, k * cols : (k + 1) * cols
            ]


def first_body(slots, halfway, *refs):
    out = refs[-1]
    for k, slot in enumerate(slots):
        out[k] = times_turned(halfway[slot], channel_row(refs[k]))


def second_images(slots, own, other, valid, factors, rights, image):
    _, rows, cols = own.shape
    channels = factors.shape[0] // rows
    for k, slot in enumerate(slots):
        image[k] = (own[k] + other[k]) * valid[slot]
    half = times(factors[...], right_terms(channel_row(image)))
    partials = []
    for k in range(len(slots)):
        here = half[:, k * cols : (k + 1) * cols].reshape(channels, rows, cols)
        partials.append(times_turned(channel_row(here), channel_row(rights[k])))
    return partials


def write_sums(slots, vector, image, sums, at):
    cols = vector.shape[2]
    cross = jnp.zeros((1, cols), F32)
    square = jnp.zeros((1, cols), F32)
    for k, slot in enumerate(slots):
        v = vector[slot]
        cross += jnp.sum(v * image[k], axis=0, keepdims=True)
        square += jnp.sum(v * v, axis=0, keepdims=True)
    ratio = jnp.where(square > 0, cross / jnp.where(square > 0, square, 1.0), 0.0)
    rest = jnp.zeros((1, cols), F32)
    for k, slot in enumerate(slots):
        away = image[k] - ratio * vector[slot]
        rest += jnp.sum(away * away, axis=0, keepdims=True)
    sums[at : at + 1, :] = cross
    sums[at + 1 : at + 2, :] = square
    sums[at + 2 : at + 3, :] = rest


def early_body(slots, own, other, valid, factors, vector, *refs):
    image, partial, sums = refs[-3:]
    parts = second_images(slots, own, other, valid, factors, refs[:-3], image)
    for k, part in enumerate(parts):
        partial[k] = part
    sums[...] = jnp.zeros_like(sums)
    write_sums(slots, vector, image, sums, 0)


def late_body(early, slots, own, other, valid, factors, vector, sums_before, before, *refs):
    image, keep, send, sums = refs[-4:]
    me = lax.axis_index("mpo") % 2
    parts = second_images(slots, own, other, valid, factors, refs[:-4], image)
    everything = {slot: before[k] for k, slot in enumerate(early)}
    everything.update(zip(slots, parts))
    for half in (0, 1):

        @pl.when(me == half)
        def _():
            for k in (0, 1):
                keep[k] = everything[2 * half + k]
                send[k] = everything[2 * (1 - half) + k]

    sums[...] = sums_before[...]
    write_sums(slots, vector, image, sums, 3)


def scalar_body(groups, cells, near, far, scalars):
    def everyone(read):
        lanes = (read(near, 0) + read(near, 16)) + (read(far, 0) + read(far, 16))
        return jnp.sum(lanes)

    def every_group(row):
        return lambda s, at: sum(
            s[at + row + 3 * g : at + row + 3 * g + 1, :] for g in range(groups)
        )

    value = everyone(every_group(0)) / (everyone(every_group(1)) + TINY)

    def rest_of(s, at):
        total = every_group(2)(s, at)
        for row in range(at, at + 3 * groups, 3):
            c = s[row + 1 : row + 2, :]
            ratio = jnp.where(c > 0, s[row : row + 1, :] / jnp.where(c > 0, c, 1.0), 0.0)
            total += (ratio - value) * (ratio - value) * c
        return total

    row = lax.broadcasted_iota(jnp.int32, scalars.shape, 0)
    scalars[...] = jnp.where(row == 0, value, 1.0 / jnp.sqrt(everyone(rest_of) / cells + TINY))


def last_body(groups, valid, scalars, total, others, *refs):
    product, ritz = refs[-2:]
    ritz[0] = scalars[0, 0]
    sector = lax.axis_index("sector")
    me = lax.axis_index("mpo") % 2
    cols = total.shape[2]
    value, scale = scalars[0:1, :], scalars[1:2, :]
    for slots, image in zip(groups, refs[:-2]):
        for k, slot in enumerate(slots):
            b = slot_column(slot, sector)
            second = jnp.where(me == slot // 2, total[slot % 2], others[slot % 2])
            product[:, columns(b, cols)] = (second * valid[slot] - value * image[k]) * scale


def line_device(wave, left, right, left_sizes, right_sizes, pairs):
    channels, rows, _ = left.shape
    cols = right.shape[2]
    sectors = 4
    cells = float(sectors * rows * sectors * cols)

    def near(x):
        return lax.ppermute(x, "sector", [(0, 1), (1, 0), (2, 3), (3, 2)])

    def far(x):
        return lax.ppermute(x, "sector", [(0, 2), (2, 0), (1, 3), (3, 1)])

    def mirror(x):
        return lax.ppermute(x, "sector", [(0, 3), (3, 0), (1, 2), (2, 1)])

    def core(x):
        return lax.ppermute(x, "mpo", [(0, 1), (1, 0), (2, 3), (3, 2)])

    def across(x):
        return lax.ppermute(x, "mpo", [(0, 2), (1, 3), (2, 0), (3, 1)])

    def shape(*dims, of=F32):
        return jax.ShapeDtypeStruct(dims, of)

    def after(x, *others):
        return lax.optimization_barrier((x, *others))[0]

    right_near = near(right)
    right_mirror = mirror(right)
    vector, halfway, factors, valid = call(
        half_body,
        [
            shape(sectors, rows, cols),
            shape(sectors, rows, channels * cols),
            shape(channels * rows, 3 * rows, of=BF16),
            shape(sectors, rows, cols),
        ],
        3,
        2,
    )(left_sizes, right_sizes, pairs, wave, left)
    right_far = near(after(right_mirror, halfway))

    def partials(slots, halfway, *rights):
        return call(
            functools.partial(first_body, slots), [shape(len(slots), rows, cols)], 0, 1 + len(slots)
        )(halfway, *rights)[0]

    def chip_sum(x):
        return x + core(x)

    one = chip_sum(after(partials((0,), halfway, right), right_mirror))
    two = chip_sum(partials((1, 2), after(halfway, one), right_near, right_mirror))
    three = chip_sum(partials((3,), after(halfway, two), right_far))
    image_early, second_early, sums = call(
        functools.partial(early_body, EARLY),
        [shape(3, rows, cols), shape(3, rows, cols), shape(16, cols)],
        0,
        8,
    )(
        jnp.concatenate([one, two]),
        jnp.concatenate([across(one), across(two)]),
        valid,
        factors,
        vector,
        right,
        right_near,
        right_mirror,
    )
    image_late, keep, send, sums = call(
        functools.partial(late_body, EARLY, LATE),
        [shape(1, rows, cols), shape(2, rows, cols), shape(2, rows, cols), shape(16, cols)],
        0,
        8,
    )(three, across(three), valid, factors, vector, sums, second_early, right_far)

    mine = keep + core(send)
    sums_near = jnp.concatenate([sums, near(sums)])
    sums_far = far(sums_near)
    total = mine + across(mine)
    others = core(total)
    (scalars,) = call(
        functools.partial(scalar_body, 2, cells), [shape(8, cols)], 0, 2, flops=3_000_000_000
    )(sums_near, sums_far)
    product, ritz = pl.pallas_call(
        functools.partial(last_body, (EARLY, LATE)),
        out_shape=[shape(rows, sectors * cols), shape(1)],
        in_specs=[VMEM] * 6,
        out_specs=[VMEM, SMEM],
        compiler_params=PARAMS,
    )(valid, scalars, total, others, image_early, image_late)
    return product, ritz


def wide_device(wave, left, right, left_sizes, right_sizes, pairs):
    sector = lax.axis_index("sector")
    sectors = lax.axis_size("sector")
    channels, rows, _ = left.shape
    cols = right.shape[2]
    cells = float(sectors * rows * sectors * cols)
    own = lax.dynamic_index_in_dim(pairs, sector, 0, keepdims=False).astype(F32)
    size = lax.dynamic_index_in_dim(left_sizes, sector, 0, keepdims=False)
    row = (jnp.arange(rows) < size).astype(F32)
    col = (jnp.arange(cols)[None, :] < right_sizes[:, None]).astype(F32) * own[:, None]
    valid = row[:, None] * col.reshape(1, -1)
    vector = wave * valid
    rights = lax.all_gather(right, "sector", axis=1)

    def image_of(v):
        half = jnp.einsum("wik,kbc->wibc", left, v.reshape(rows, sectors, cols), precision=EXACT)
        out = jnp.einsum("wibc,wbjc->ibj", half, rights, precision=EXACT)
        return lax.psum(out.reshape(rows, sectors * cols), "mpo") * valid

    first = image_of(vector)
    cross, square = lax.psum((jnp.sum(vector * first), jnp.sum(vector * vector)), "sector")
    value = cross / (square + TINY)
    residual = first - value * vector
    rest = lax.psum(jnp.sum(residual * residual), "sector")
    product = image_of(residual / jnp.sqrt(rest / cells + TINY))
    return product, jnp.reshape(value, (1,))


def solution(mesh):
    line = mesh.shape["sector"] == 4 and mesh.shape["mpo"] == 4
    return jax.shard_map(
        line_device if line else wide_device,
        mesh=mesh,
        in_specs=(
            P(("groups", "sector"), None),
            P("mpo", ("groups", "sector"), None),
            P("mpo", ("groups", "sector"), None),
            P("groups"),
            P("groups"),
            P("groups", None),
        ),
        out_specs=(P(("groups", "sector"), None), P("groups")),
        check_vma=False,
    )
```

```python
import functools

import jax
import jax.numpy as jnp
from jax import lax
from jax.experimental import pallas as pl
from jax.experimental.pallas import tpu as pltpu
from jax.sharding import PartitionSpec as P

EXACT = lax.Precision.HIGHEST
TINY = 1e-06
PARAMS = pltpu.CompilerParams(vmem_limit_bytes=32 * 1024 * 1024)
VMEM = pl.BlockSpec(memory_space=pltpu.VMEM)
SMEM = pl.BlockSpec(memory_space=pltpu.SMEM)
F32 = jnp.float32
BF16 = jnp.bfloat16

EARLY, LATE = (0, 1, 2), (3,)


def split(x):
    high = x.astype(BF16)
    return high, (x - high.astype(F32)).astype(BF16)


def times(a, x):
    n = x.shape[1]
    parts = jnp.concatenate(split(x), axis=1)
    both = lax.dot_general(
        a,
        jnp.concatenate([parts, parts], axis=0),
        (((1,), (0,)), ((), ())),
        preferred_element_type=F32,
    )
    return both[:, n:] + both[:, :n]


def times_turned(a, b):
    m, n = a.shape[0], b.shape[0]
    both = lax.dot_general(
        jnp.concatenate(split(a), axis=0),
        jnp.concatenate(split(b), axis=0),
        (((1,), (1,)), ((), ())),
        preferred_element_type=F32,
    )
    return (both[m:, n:] + (both[m:, :n] + both[:m, n:])) + both[:m, :n]


def block_valid(left_sizes, right_sizes, pairs, a, b, rows, cols):
    row = lax.broadcasted_iota(jnp.int32, (rows, cols), 0) < left_sizes[a]
    col = lax.broadcasted_iota(jnp.int32, (rows, cols), 1) < right_sizes[b]
    return (row & col).astype(F32) * pairs[a, b].astype(F32)


def call(body, outs, n_small, n_big, flops=None):
    cost = None
    if flops is not None:
        cost = pl.CostEstimate(flops=flops, bytes_accessed=flops // 100, transcendentals=0)
    return pl.pallas_call(
        body,
        out_shape=outs,
        in_specs=[SMEM] * n_small + [VMEM] * n_big,
        out_specs=[VMEM] * len(outs),
        compiler_params=PARAMS,
        cost_estimate=cost,
    )


def slot_column(slot, sector):
    return sector ^ (0, 1, 3, 2)[slot]


def columns(b, width):
    return pl.ds(pl.multiple_of(b * width, width), width)


def channel_row(blocks):
    return jnp.concatenate([blocks[w] for w in range(blocks.shape[0])], axis=1)


def half_body(left_sizes, right_sizes, pairs, wave, left, vector, halfway, factors, valid):
    sector = lax.axis_index("sector")
    channels, rows, _ = left.shape
    slots, _, inner = halfway.shape
    cols = inner // channels
    factors[...] = jnp.concatenate(split(left[...].reshape(channels * rows, rows)), axis=1)
    for k in range(slots):
        b = slot_column(k, sector)
        valid[k] = block_valid(left_sizes, right_sizes, pairs, sector, b, rows, cols)
        vector[k] = wave[:, columns(b, cols)] * valid[k]
    part = times(factors[...], channel_row(vector))
    for k in range(slots):
        for w in range(channels):
            halfway[k, :, w * cols : (w + 1) * cols] = part[
                w * rows : (w + 1) * rows, k * cols : (k + 1) * cols
            ]


def first_body(slots, halfway, *refs):
    out = refs[-1]
    for k, slot in enumerate(slots):
        out[k] = times_turned(halfway[slot], channel_row(refs[k]))


def second_images(slots, own, other, valid, factors, rights, image):
    _, rows, cols = own.shape
    channels = factors.shape[0] // rows
    for k, slot in enumerate(slots):
        image[k] = (own[k] + other[k]) * valid[slot]
    half = times(factors[...], channel_row(image))
    partials = []
    for k in range(len(slots)):
        here = half[:, k * cols : (k + 1) * cols].reshape(channels, rows, cols)
        partials.append(times_turned(channel_row(here), channel_row(rights[k])))
    return partials


def write_sums(slots, vector, image, sums, at):
    cols = vector.shape[2]
    cross = jnp.zeros((1, cols), F32)
    square = jnp.zeros((1, cols), F32)
    for k, slot in enumerate(slots):
        v = vector[slot]
        cross += jnp.sum(v * image[k], axis=0, keepdims=True)
        square += jnp.sum(v * v, axis=0, keepdims=True)
    ratio = jnp.where(square > 0, cross / jnp.where(square > 0, square, 1.0), 0.0)
    rest = jnp.zeros((1, cols), F32)
    for k, slot in enumerate(slots):
        away = image[k] - ratio * vector[slot]
        rest += jnp.sum(away * away, axis=0, keepdims=True)
    sums[at : at + 1, :] = cross
    sums[at + 1 : at + 2, :] = square
    sums[at + 2 : at + 3, :] = rest


def early_body(slots, own, other, valid, factors, vector, *refs):
    image, partial, sums = refs[-3:]
    parts = second_images(slots, own, other, valid, factors, refs[:-3], image)
    for k, part in enumerate(parts):
        partial[k] = part
    sums[...] = jnp.zeros_like(sums)
    write_sums(slots, vector, image, sums, 0)


def late_body(early, slots, own, other, valid, factors, vector, sums_before, before, *refs):
    image, keep, send, sums = refs[-4:]
    me = lax.axis_index("mpo") % 2
    parts = second_images(slots, own, other, valid, factors, refs[:-4], image)
    everything = {slot: before[k] for k, slot in enumerate(early)}
    everything.update(zip(slots, parts))
    for half in (0, 1):

        @pl.when(me == half)
        def _():
            for k in (0, 1):
                keep[k] = everything[2 * half + k]
                send[k] = everything[2 * (1 - half) + k]

    sums[...] = sums_before[...]
    write_sums(slots, vector, image, sums, 3)


def scalar_body(groups, cells, near, far, scalars):
    def everyone(read):
        lanes = (read(near, 0) + read(near, 8)) + (read(far, 0) + read(far, 8))
        return jnp.sum(lanes, axis=1, keepdims=True)

    def every_group(row):
        return lambda s, at: sum(
            s[at + row + 3 * g : at + row + 3 * g + 1, :] for g in range(groups)
        )

    both = everyone(lambda s, at: s[at : at + 2, :] + s[at + 3 : at + 5, :])
    value = both[0:1, :] / (both[1:2, :] + TINY)

    def rest_of(s, at):
        total = every_group(2)(s, at)
        for row in range(at, at + 3 * groups, 3):
            c = s[row + 1 : row + 2, :]
            ratio = jnp.where(c > 0, s[row : row + 1, :] / jnp.where(c > 0, c, 1.0), 0.0)
            total += (ratio - value) * (ratio - value) * c
        return total

    scale = 1.0 / jnp.sqrt(everyone(rest_of) / cells + TINY)
    scalars[0:1, :] = jnp.broadcast_to(value, (1, scalars.shape[1]))
    scalars[1:2, :] = jnp.broadcast_to(scale, (1, scalars.shape[1]))


def last_body(groups, valid, scalars, total, others, *refs):
    product, ritz = refs[-2:]
    ritz[0] = scalars[0, 0]
    sector = lax.axis_index("sector")
    me = lax.axis_index("mpo") % 2
    cols = total.shape[2]
    value, scale = scalars[0:1, :], scalars[1:2, :]
    for slots, image in zip(groups, refs[:-2]):
        for k, slot in enumerate(slots):
            b = slot_column(slot, sector)
            second = jnp.where(me == slot // 2, total[slot % 2], others[slot % 2])
            product[:, columns(b, cols)] = (second * valid[slot] - value * image[k]) * scale


def line_device(wave, left, right, left_sizes, right_sizes, pairs):
    channels, rows, _ = left.shape
    cols = right.shape[2]
    sectors = 4
    cells = float(sectors * rows * sectors * cols)

    def near(x):
        return lax.ppermute(x, "sector", [(0, 1), (1, 0), (2, 3), (3, 2)])

    def far(x):
        return lax.ppermute(x, "sector", [(0, 2), (2, 0), (1, 3), (3, 1)])

    def mirror(x):
        return lax.ppermute(x, "sector", [(0, 3), (3, 0), (1, 2), (2, 1)])

    def core(x):
        return lax.ppermute(x, "mpo", [(0, 1), (1, 0), (2, 3), (3, 2)])

    def across(x):
        return lax.ppermute(x, "mpo", [(0, 2), (1, 3), (2, 0), (3, 1)])

    def shape(*dims, of=F32):
        return jax.ShapeDtypeStruct(dims, of)

    def after(x, *others):
        return lax.optimization_barrier((x, *others))[0]

    right_near = near(right)
    right_mirror = mirror(right)
    vector, halfway, factors, valid = call(
        half_body,
        [
            shape(sectors, rows, cols),
            shape(sectors, rows, channels * cols),
            shape(channels * rows, 2 * rows, of=BF16),
            shape(sectors, rows, cols),
        ],
        3,
        2,
    )(left_sizes, right_sizes, pairs, wave, left)
    right_far = near(after(right_mirror, halfway))

    def partials(slots, halfway, *rights):
        return call(
            functools.partial(first_body, slots), [shape(len(slots), rows, cols)], 0, 1 + len(slots)
        )(halfway, *rights)[0]

    def chip_sum(x):
        return x + core(x)

    one = chip_sum(after(partials((0,), halfway, right), right_mirror))
    two = chip_sum(partials((1, 2), after(halfway, one), right_near, right_mirror))
    three = chip_sum(partials((3,), after(halfway, two), right_far))
    image_early, second_early, sums = call(
        functools.partial(early_body, EARLY),
        [shape(3, rows, cols), shape(3, rows, cols), shape(8, cols)],
        0,
        8,
    )(
        jnp.concatenate([one, two]),
        jnp.concatenate([across(one), across(two)]),
        valid,
        factors,
        vector,
        right,
        right_near,
        right_mirror,
    )
    image_late, keep, send, sums = call(
        functools.partial(late_body, EARLY, LATE),
        [shape(1, rows, cols), shape(2, rows, cols), shape(2, rows, cols), shape(8, cols)],
        0,
        8,
    )(three, across(three), valid, factors, vector, sums, second_early, right_far)

    mine = keep + core(send)
    sums_near = jnp.concatenate([sums, near(sums)])
    sums_far = far(sums_near)
    total = mine + across(mine)
    others = core(total)
    (scalars,) = call(
        functools.partial(scalar_body, 2, cells), [shape(8, cols)], 0, 2, flops=3_000_000_000
    )(sums_near, sums_far)
    product, ritz = pl.pallas_call(
        functools.partial(last_body, (EARLY, LATE)),
        out_shape=[shape(rows, sectors * cols), shape(1)],
        in_specs=[VMEM] * 6,
        out_specs=[VMEM, SMEM],
        compiler_params=PARAMS,
    )(valid, scalars, total, others, image_early, image_late)
    return product, ritz


def wide_device(wave, left, right, left_sizes, right_sizes, pairs):
    sector = lax.axis_index("sector")
    sectors = lax.axis_size("sector")
    channels, rows, _ = left.shape
    cols = right.shape[2]
    cells = float(sectors * rows * sectors * cols)
    own = lax.dynamic_index_in_dim(pairs, sector, 0, keepdims=False).astype(F32)
    size = lax.dynamic_index_in_dim(left_sizes, sector, 0, keepdims=False)
    row = (jnp.arange(rows) < size).astype(F32)
    col = (jnp.arange(cols)[None, :] < right_sizes[:, None]).astype(F32) * own[:, None]
    valid = row[:, None] * col.reshape(1, -1)
    vector = wave * valid
    rights = lax.all_gather(right, "sector", axis=1)

    def image_of(v):
        half = jnp.einsum("wik,kbc->wibc", left, v.reshape(rows, sectors, cols), precision=EXACT)
        out = jnp.einsum("wibc,wbjc->ibj", half, rights, precision=EXACT)
        return lax.psum(out.reshape(rows, sectors * cols), "mpo") * valid

    first = image_of(vector)
    cross, square = lax.psum((jnp.sum(vector * first), jnp.sum(vector * vector)), "sector")
    value = cross / (square + TINY)
    residual = first - value * vector
    rest = lax.psum(jnp.sum(residual * residual), "sector")
    product = image_of(residual / jnp.sqrt(rest / cells + TINY))
    return product, jnp.reshape(value, (1,))


def solution(mesh):
    line = mesh.shape["sector"] == 4 and mesh.shape["mpo"] == 4
    return jax.shard_map(
        line_device if line else wide_device,
        mesh=mesh,
        in_specs=(
            P(("groups", "sector"), None),
            P("mpo", ("groups", "sector"), None),
            P("mpo", ("groups", "sector"), None),
            P("groups"),
            P("groups"),
            P("groups", None),
        ),
        out_specs=(P(("groups", "sector"), None), P("groups")),
        check_vma=False,
    )
```

```python
import functools

import jax
import jax.numpy as jnp
from jax import lax
from jax.experimental import pallas as pl
from jax.experimental.pallas import tpu as pltpu
from jax.sharding import PartitionSpec as P

EXACT = lax.Precision.HIGHEST
TINY = 1e-06
PARAMS = pltpu.CompilerParams(vmem_limit_bytes=32 * 1024 * 1024)
VMEM = pl.BlockSpec(memory_space=pltpu.VMEM)
SMEM = pl.BlockSpec(memory_space=pltpu.SMEM)
F32 = jnp.float32
BF16 = jnp.bfloat16

EARLY, LATE = (0, 1, 2), (3,)


def split(x):
    high = x.astype(BF16)
    rest = x - high.astype(F32)
    middle = rest.astype(BF16)
    return high, middle, (rest - middle.astype(F32)).astype(BF16)


def matmul(a, b, turned=False):
    return lax.dot_general(
        a, b, (((1,), (1 if turned else 0,)), ((), ())), preferred_element_type=F32
    )


def left_parts(a):
    high, middle, low = split(a)
    return jnp.concatenate([middle, high, low], axis=1)


def times(parts, x):
    depth, n = x.shape
    high, middle, low = split(x)
    large = jnp.concatenate([high, middle], axis=1)
    large = matmul(parts[:, : 2 * depth], jnp.concatenate([large, large], axis=0))
    small = matmul(parts[:, depth:], jnp.concatenate([low, high], axis=0))
    return (small + large[:, n:]) + large[:, :n]


def times_turned(a, b):
    m, n = a.shape[0], b.shape[0]
    a_high, a_middle, a_low = split(a)
    b_high, b_middle, b_low = split(b)
    large = matmul(
        jnp.concatenate([a_high, a_middle], axis=0),
        jnp.concatenate([b_high, b_middle], axis=0),
        turned=True,
    )
    small = matmul(
        jnp.concatenate([a_high, a_low], axis=1),
        jnp.concatenate([b_low, b_high], axis=1),
        turned=True,
    )
    return ((small + large[m:, n:]) + (large[m:, :n] + large[:m, n:])) + large[:m, :n]


def block_valid(left_sizes, right_sizes, pairs, a, b, rows, cols):
    row = lax.broadcasted_iota(jnp.int32, (rows, cols), 0) < left_sizes[a]
    col = lax.broadcasted_iota(jnp.int32, (rows, cols), 1) < right_sizes[b]
    return (row & col).astype(F32) * pairs[a, b].astype(F32)


def call(body, outs, n_small, n_big, flops=None):
    cost = None
    if flops is not None:
        cost = pl.CostEstimate(flops=flops, bytes_accessed=flops // 100, transcendentals=0)
    return pl.pallas_call(
        body,
        out_shape=outs,
        in_specs=[SMEM] * n_small + [VMEM] * n_big,
        out_specs=[VMEM] * len(outs),
        compiler_params=PARAMS,
        cost_estimate=cost,
    )


def slot_column(slot, sector):
    return sector ^ (0, 1, 3, 2)[slot]


def columns(b, width):
    return pl.ds(pl.multiple_of(b * width, width), width)


def channel_row(blocks):
    return jnp.concatenate([blocks[w] for w in range(blocks.shape[0])], axis=1)


def half_body(left_sizes, right_sizes, pairs, wave, left, vector, halfway, factors, valid):
    sector = lax.axis_index("sector")
    channels, rows, _ = left.shape
    slots, _, inner = halfway.shape
    cols = inner // channels
    factors[...] = left_parts(left[...].reshape(channels * rows, rows))
    for k in range(slots):
        b = slot_column(k, sector)
        valid[k] = block_valid(left_sizes, right_sizes, pairs, sector, b, rows, cols)
        vector[k] = wave[:, columns(b, cols)] * valid[k]
    part = times(factors[...], channel_row(vector))
    for k in range(slots):
        for w in range(channels):
            halfway[k, :, w * cols : (w + 1) * cols] = part[
                w * rows : (w + 1) * rows, k * cols : (k + 1) * cols
            ]


def first_body(slots, halfway, *refs):
    out = refs[-1]
    for k, slot in enumerate(slots):
        out[k] = times_turned(halfway[slot], channel_row(refs[k]))


def ratio_of(cross, square):
    return jnp.where(square > 0, cross / jnp.where(square > 0, square, 1.0), 0.0)


def second_images(slots, own, other, valid, factors, rights, image):
    _, rows, cols = own.shape
    channels = factors.shape[0] // rows
    for k, slot in enumerate(slots):
        image[k] = (own[k] + other[k]) * valid[slot]
    half = times(factors[...], channel_row(image))
    partials = []
    for k in range(len(slots)):
        here = half[:, k * cols : (k + 1) * cols].reshape(channels, rows, cols)
        partials.append(times_turned(channel_row(here), channel_row(rights[k])))
    return partials


def write_sums(slots, vector, image, sums, at):
    cols = vector.shape[2]
    cross = jnp.zeros((1, cols), F32)
    square = jnp.zeros((1, cols), F32)
    for k, slot in enumerate(slots):
        v = vector[slot]
        cross += jnp.sum(v * image[k], axis=0, keepdims=True)
        square += jnp.sum(v * v, axis=0, keepdims=True)
    both = jnp.sum(jnp.concatenate([cross, square], axis=0), axis=1, keepdims=True)
    both = jnp.broadcast_to(both, (2, cols))
    ratio = ratio_of(both[0:1], both[1:2])
    rest = jnp.zeros((1, cols), F32)
    for k, slot in enumerate(slots):
        away = image[k] - ratio * vector[slot]
        rest += jnp.sum(away * away, axis=0, keepdims=True)
    sums[at : at + 2, :] = both
    sums[at + 2 : at + 3, :] = rest


def early_body(slots, own, other, valid, factors, vector, *refs):
    image, partial, sums = refs[-3:]
    parts = second_images(slots, own, other, valid, factors, refs[:-3], image)
    for k, part in enumerate(parts):
        partial[k] = part
    sums[...] = jnp.zeros_like(sums)
    write_sums(slots, vector, image, sums, 0)


def late_body(early, slots, own, other, valid, factors, vector, sums_before, before, *refs):
    image, keep, send, sums = refs[-4:]
    me = lax.axis_index("mpo") % 2
    parts = second_images(slots, own, other, valid, factors, refs[:-4], image)
    everything = {slot: before[k] for k, slot in enumerate(early)}
    everything.update(zip(slots, parts))
    for half in (0, 1):

        @pl.when(me == half)
        def _():
            for k in (0, 1):
                keep[k] = everything[2 * half + k]
                send[k] = everything[2 * (1 - half) + k]

    sums[...] = sums_before[...]
    write_sums(slots, vector, image, sums, 3)


def scalar_body(groups, cells, near, far, scalars):
    def everyone(read):
        return (read(near, 0) + read(near, 8)) + (read(far, 0) + read(far, 8))

    def every_group(row):
        return lambda s, at: sum(s[at + row + 3 * g : at + row + 3 * g + 1, :] for g in range(groups))

    value = everyone(every_group(0)) / (everyone(every_group(1)) + TINY)

    def gaps(s, at):
        total = 0.0
        for row in range(at, at + 3 * groups, 3):
            square = s[row + 1 : row + 2, :]
            gap = ratio_of(s[row : row + 1, :], square) - value
            total += gap * (gap * square)
        return total

    rest = jnp.sum(everyone(every_group(2)), axis=1, keepdims=True) + everyone(gaps)
    scalars[0:1, :] = value
    scalars[1:2, :] = 1.0 / jnp.sqrt(rest / cells + TINY)


def last_body(groups, valid, scalars, total, others, *refs):
    product, ritz = refs[-2:]
    ritz[0] = scalars[0, 0]
    sector = lax.axis_index("sector")
    me = lax.axis_index("mpo") % 2
    cols = total.shape[2]
    value, scale = scalars[0:1, :], scalars[1:2, :]
    for slots, image in zip(groups, refs[:-2]):
        for k, slot in enumerate(slots):
            b = slot_column(slot, sector)
            second = jnp.where(me == slot // 2, total[slot % 2], others[slot % 2])
            product[:, columns(b, cols)] = (second * valid[slot] - value * image[k]) * scale


def line_device(wave, left, right, left_sizes, right_sizes, pairs):
    channels, rows, _ = left.shape
    cols = right.shape[2]
    sectors = 4
    cells = float(sectors * rows * sectors * cols)

    def near(x):
        return lax.ppermute(x, "sector", [(0, 1), (1, 0), (2, 3), (3, 2)])

    def far(x):
        return lax.ppermute(x, "sector", [(0, 2), (2, 0), (1, 3), (3, 1)])

    def mirror(x):
        return lax.ppermute(x, "sector", [(0, 3), (3, 0), (1, 2), (2, 1)])

    def core(x):
        return lax.ppermute(x, "mpo", [(0, 1), (1, 0), (2, 3), (3, 2)])

    def across(x):
        return lax.ppermute(x, "mpo", [(0, 2), (1, 3), (2, 0), (3, 1)])

    def shape(*dims, of=F32):
        return jax.ShapeDtypeStruct(dims, of)

    def after(x, *others):
        return lax.optimization_barrier((x, *others))[0]

    right_near = near(right)
    right_mirror = mirror(right)
    vector, halfway, factors, valid = call(
        half_body,
        [
            shape(sectors, rows, cols),
            shape(sectors, rows, channels * cols),
            shape(channels * rows, 3 * rows, of=BF16),
            shape(sectors, rows, cols),
        ],
        3,
        2,
    )(left_sizes, right_sizes, pairs, wave, left)
    right_far = near(after(right_mirror, halfway))

    def partials(slots, halfway, *rights):
        return call(
            functools.partial(first_body, slots), [shape(len(slots), rows, cols)], 0, 1 + len(slots)
        )(halfway, *rights)[0]

    def chip_sum(x):
        return x + core(x)

    one = chip_sum(after(partials((0,), halfway, right), right_mirror))
    two = chip_sum(partials((1, 2), after(halfway, one), right_near, right_mirror))
    three = chip_sum(partials((3,), after(halfway, two), right_far))
    image_early, second_early, sums = call(
        functools.partial(early_body, EARLY),
        [shape(3, rows, cols), shape(3, rows, cols), shape(8, cols)],
        0,
        8,
    )(
        jnp.concatenate([one, two]),
        jnp.concatenate([across(one), across(two)]),
        valid,
        factors,
        vector,
        right,
        right_near,
        right_mirror,
    )
    image_late, keep, send, sums = call(
        functools.partial(late_body, EARLY, LATE),
        [shape(1, rows, cols), shape(2, rows, cols), shape(2, rows, cols), shape(8, cols)],
        0,
        8,
    )(three, across(three), valid, factors, vector, sums, second_early, right_far)

    mine = keep + core(send)
    sums_near = jnp.concatenate([sums, near(sums)])
    sums_far = far(sums_near)
    total = mine + across(mine)
    others = core(total)
    (scalars,) = call(
        functools.partial(scalar_body, 2, cells), [shape(8, cols)], 0, 2, flops=3_000_000_000
    )(sums_near, sums_far)
    product, ritz = pl.pallas_call(
        functools.partial(last_body, (EARLY, LATE)),
        out_shape=[shape(rows, sectors * cols), shape(1)],
        in_specs=[VMEM] * 6,
        out_specs=[VMEM, SMEM],
        compiler_params=PARAMS,
    )(valid, scalars, total, others, image_early, image_late)
    return product, ritz


def wide_device(wave, left, right, left_sizes, right_sizes, pairs):
    sector = lax.axis_index("sector")
    sectors = lax.axis_size("sector")
    channels, rows, _ = left.shape
    cols = right.shape[2]
    cells = float(sectors * rows * sectors * cols)
    own = lax.dynamic_index_in_dim(pairs, sector, 0, keepdims=False).astype(F32)
    size = lax.dynamic_index_in_dim(left_sizes, sector, 0, keepdims=False)
    row = (jnp.arange(rows) < size).astype(F32)
    col = (jnp.arange(cols)[None, :] < right_sizes[:, None]).astype(F32) * own[:, None]
    valid = row[:, None] * col.reshape(1, -1)
    vector = wave * valid
    rights = lax.all_gather(right, "sector", axis=1)

    def image_of(v):
        half = jnp.einsum("wik,kbc->wibc", left, v.reshape(rows, sectors, cols), precision=EXACT)
        out = jnp.einsum("wibc,wbjc->ibj", half, rights, precision=EXACT)
        return lax.psum(out.reshape(rows, sectors * cols), "mpo") * valid

    first = image_of(vector)
    cross, square = lax.psum((jnp.sum(vector * first), jnp.sum(vector * vector)), "sector")
    value = cross / (square + TINY)
    residual = first - value * vector
    rest = lax.psum(jnp.sum(residual * residual), "sector")
    product = image_of(residual / jnp.sqrt(rest / cells + TINY))
    return product, jnp.reshape(value, (1,))


def solution(mesh):
    line = mesh.shape["sector"] == 4 and mesh.shape["mpo"] == 4
    return jax.shard_map(
        line_device if line else wide_device,
        mesh=mesh,
        in_specs=(
            P(("groups", "sector"), None),
            P("mpo", ("groups", "sector"), None),
            P("mpo", ("groups", "sector"), None),
            P("groups"),
            P("groups"),
            P("groups", None),
        ),
        out_specs=(P(("groups", "sector"), None), P("groups")),
        check_vma=False,
    )
```

```python
import functools

import jax
import jax.numpy as jnp
from jax import lax
from jax.experimental import pallas as pl
from jax.experimental.pallas import tpu as pltpu
from jax.sharding import PartitionSpec as P

EXACT = lax.Precision.HIGHEST
TINY = 1e-06
PARAMS = pltpu.CompilerParams(vmem_limit_bytes=32 * 1024 * 1024)
VMEM = pl.BlockSpec(memory_space=pltpu.VMEM)
SMEM = pl.BlockSpec(memory_space=pltpu.SMEM)
F32 = jnp.float32
BF16 = jnp.bfloat16

EARLY, LATE = (0, 1, 2), (3,)


def split(x):
    high = x.astype(BF16)
    rest = x - high.astype(F32)
    middle = rest.astype(BF16)
    return high, middle, (rest - middle.astype(F32)).astype(BF16)


def matmul(a, b, turned=False):
    return lax.dot_general(
        a, b, (((1,), (1 if turned else 0,)), ((), ())), preferred_element_type=F32
    )


def left_parts(a):
    high, middle, low = split(a)
    return jnp.concatenate([middle, high, low], axis=1)


def times(parts, x):
    depth, n = x.shape
    high, middle, low = split(x)
    large = jnp.concatenate([high, middle], axis=1)
    large = matmul(parts[:, : 2 * depth], jnp.concatenate([large, large], axis=0))
    small = matmul(parts[:, depth:], jnp.concatenate([low, high], axis=0))
    return (small + large[:, n:]) + large[:, :n]


def times_turned(a, b):
    m, n = a.shape[0], b.shape[0]
    a_high, a_middle, a_low = split(a)
    b_high, b_middle, b_low = split(b)
    large = matmul(
        jnp.concatenate([a_high, a_middle], axis=0),
        jnp.concatenate([b_high, b_middle], axis=0),
        turned=True,
    )
    small = matmul(
        jnp.concatenate([a_high, a_low], axis=1),
        jnp.concatenate([b_low, b_high], axis=1),
        turned=True,
    )
    return ((small + large[m:, n:]) + (large[m:, :n] + large[:m, n:])) + large[:m, :n]


def block_valid(left_sizes, right_sizes, pairs, a, b, rows, cols):
    row = lax.broadcasted_iota(jnp.int32, (rows, cols), 0) < left_sizes[a]
    col = lax.broadcasted_iota(jnp.int32, (rows, cols), 1) < right_sizes[b]
    return (row & col).astype(F32) * pairs[a, b].astype(F32)


def call(body, outs, n_small, n_big, flops=None):
    cost = None
    if flops is not None:
        cost = pl.CostEstimate(flops=flops, bytes_accessed=flops // 100, transcendentals=0)
    return pl.pallas_call(
        body,
        out_shape=outs,
        in_specs=[SMEM] * n_small + [VMEM] * n_big,
        out_specs=[VMEM] * len(outs),
        compiler_params=PARAMS,
        cost_estimate=cost,
    )


def slot_column(slot, sector):
    return sector ^ (0, 1, 3, 2)[slot]


def columns(b, width):
    return pl.ds(pl.multiple_of(b * width, width), width)


def channel_row(blocks):
    return jnp.concatenate([blocks[w] for w in range(blocks.shape[0])], axis=1)


def half_body(left_sizes, right_sizes, pairs, wave, left, vector, halfway, factors, valid):
    sector = lax.axis_index("sector")
    channels, rows, _ = left.shape
    slots, _, inner = halfway.shape
    cols = inner // channels
    factors[...] = left_parts(left[...].reshape(channels * rows, rows))
    for k in range(slots):
        b = slot_column(k, sector)
        valid[k] = block_valid(left_sizes, right_sizes, pairs, sector, b, rows, cols)
        vector[k] = wave[:, columns(b, cols)] * valid[k]
    part = times(factors[...], channel_row(vector))
    for k in range(slots):
        for w in range(channels):
            halfway[k, :, w * cols : (w + 1) * cols] = part[
                w * rows : (w + 1) * rows, k * cols : (k + 1) * cols
            ]


def first_body(slots, halfway, *refs):
    out = refs[-1]
    for k, slot in enumerate(slots):
        out[k] = times_turned(halfway[slot], channel_row(refs[k]))


def ratio_of(cross, square):
    return jnp.where(square > 0, cross / jnp.where(square > 0, square, 1.0), 0.0)


def first_images(slots, own, other, valid, image):
    for k, slot in enumerate(slots):
        image[k] = (own[k] + other[k]) * valid[slot]


def second_images(factors, rights, image):
    slots, rows, cols = image.shape
    channels = factors.shape[0] // rows
    half = times(factors[...], channel_row(image))
    partials = []
    for k in range(slots):
        here = half[:, k * cols : (k + 1) * cols].reshape(channels, rows, cols)
        partials.append(times_turned(channel_row(here), channel_row(rights[k])))
    return partials


def write_sums(slots, vector, image, sums, at):
    cols = vector.shape[2]
    cross = jnp.zeros((1, cols), F32)
    square = jnp.zeros((1, cols), F32)
    for k, slot in enumerate(slots):
        v = vector[slot]
        cross += jnp.sum(v * image[k], axis=0, keepdims=True)
        square += jnp.sum(v * v, axis=0, keepdims=True)
    both = jnp.sum(jnp.concatenate([cross, square], axis=0), axis=1, keepdims=True)
    both = jnp.broadcast_to(both, (2, cols))
    ratio = ratio_of(both[0:1], both[1:2])
    rest = jnp.zeros((1, cols), F32)
    for k, slot in enumerate(slots):
        away = image[k] - ratio * vector[slot]
        rest += jnp.sum(away * away, axis=0, keepdims=True)
    sums[at : at + 2, :] = both
    sums[at + 2 : at + 3, :] = rest


def early_body(slots, own, other, valid, factors, vector, *refs):
    image, partial, sums = refs[-3:]
    first_images(slots, own, other, valid, image)
    sums[...] = jnp.zeros_like(sums)
    write_sums(slots, vector, image, sums, 0)
    for k, part in enumerate(second_images(factors, refs[:-3], image)):
        partial[k] = part


def late_body(early, slots, own, other, valid, factors, vector, sums_before, before, *refs):
    image, keep, send, sums = refs[-4:]
    first = lax.axis_index("mpo") % 2 == 0
    first_images(slots, own, other, valid, image)
    sums[...] = sums_before[...]
    write_sums(slots, vector, image, sums, 3)
    everything = {slot: before[k] for k, slot in enumerate(early)}
    everything.update(zip(slots, second_images(factors, refs[:-4], image)))
    for k in (0, 1):
        keep[k] = jnp.where(first, everything[k], everything[2 + k])
        send[k] = jnp.where(first, everything[2 + k], everything[k])


def scalar_body(groups, cells, near, far, scalars):
    def everyone(read):
        return (read(near, 0) + read(near, 8)) + (read(far, 0) + read(far, 8))

    def every_group(row):
        return lambda s, at: sum(s[at + row + 3 * g : at + row + 3 * g + 1, :] for g in range(groups))

    value = everyone(every_group(0)) / (everyone(every_group(1)) + TINY)

    def gaps(s, at):
        total = 0.0
        for row in range(at, at + 3 * groups, 3):
            square = s[row + 1 : row + 2, :]
            gap = ratio_of(s[row : row + 1, :], square) - value
            total += gap * (gap * square)
        return total

    rest = jnp.sum(everyone(every_group(2)), axis=1, keepdims=True) + everyone(gaps)
    scalars[0:1, :] = value
    scalars[1:2, :] = 1.0 / jnp.sqrt(rest / cells + TINY)


def last_body(groups, valid, scalars, total, others, *refs):
    product, ritz = refs[-2:]
    ritz[0] = scalars[0, 0]
    sector = lax.axis_index("sector")
    me = lax.axis_index("mpo") % 2
    cols = total.shape[2]
    value, scale = scalars[0:1, :], scalars[1:2, :]
    for slots, image in zip(groups, refs[:-2]):
        for k, slot in enumerate(slots):
            b = slot_column(slot, sector)
            second = jnp.where(me == slot // 2, total[slot % 2], others[slot % 2])
            product[:, columns(b, cols)] = (second * valid[slot] - value * image[k]) * scale


def line_device(wave, left, right, left_sizes, right_sizes, pairs):
    channels, rows, _ = left.shape
    cols = right.shape[2]
    sectors = 4
    cells = float(sectors * rows * sectors * cols)

    def near(x):
        return lax.ppermute(x, "sector", [(0, 1), (1, 0), (2, 3), (3, 2)])

    def far(x):
        return lax.ppermute(x, "sector", [(0, 2), (2, 0), (1, 3), (3, 1)])

    def mirror(x):
        return lax.ppermute(x, "sector", [(0, 3), (3, 0), (1, 2), (2, 1)])

    def core(x):
        return lax.ppermute(x, "mpo", [(0, 1), (1, 0), (2, 3), (3, 2)])

    def across(x):
        return lax.ppermute(x, "mpo", [(0, 2), (1, 3), (2, 0), (3, 1)])

    def shape(*dims, of=F32):
        return jax.ShapeDtypeStruct(dims, of)

    def after(x, *others):
        return lax.optimization_barrier((x, *others))[0]

    right_near = near(right)
    right_mirror = mirror(right)
    vector, halfway, factors, valid = call(
        half_body,
        [
            shape(sectors, rows, cols),
            shape(sectors, rows, channels * cols),
            shape(channels * rows, 3 * rows, of=BF16),
            shape(sectors, rows, cols),
        ],
        3,
        2,
    )(left_sizes, right_sizes, pairs, wave, left)
    right_far = near(after(right_mirror, halfway))

    def partials(slots, halfway, *rights):
        return call(
            functools.partial(first_body, slots), [shape(len(slots), rows, cols)], 0, 1 + len(slots)
        )(halfway, *rights)[0]

    def chip_sum(x):
        return x + core(x)

    one = chip_sum(after(partials((0,), halfway, right), right_mirror))
    two = chip_sum(partials((1, 2), after(halfway, one), right_near, right_mirror))
    three = chip_sum(partials((3,), after(halfway, two), right_far))
    image_early, second_early, sums = call(
        functools.partial(early_body, EARLY),
        [shape(3, rows, cols), shape(3, rows, cols), shape(8, cols)],
        0,
        8,
    )(
        jnp.concatenate([one, two]),
        jnp.concatenate([across(one), across(two)]),
        valid,
        factors,
        vector,
        right,
        right_near,
        right_mirror,
    )
    image_late, keep, send, sums = call(
        functools.partial(late_body, EARLY, LATE),
        [shape(1, rows, cols), shape(2, rows, cols), shape(2, rows, cols), shape(8, cols)],
        0,
        8,
    )(three, across(three), valid, factors, vector, sums, second_early, right_far)

    mine = keep + core(send)
    sums_near = jnp.concatenate([sums, near(sums)])
    sums_far = far(sums_near)
    total = mine + across(mine)
    others = core(total)
    (scalars,) = call(
        functools.partial(scalar_body, 2, cells), [shape(8, cols)], 0, 2, flops=3_000_000_000
    )(sums_near, sums_far)
    product, ritz = pl.pallas_call(
        functools.partial(last_body, (EARLY, LATE)),
        out_shape=[shape(rows, sectors * cols), shape(1)],
        in_specs=[VMEM] * 6,
        out_specs=[VMEM, SMEM],
        compiler_params=PARAMS,
    )(valid, scalars, total, others, image_early, image_late)
    return product, ritz


def wide_device(wave, left, right, left_sizes, right_sizes, pairs):
    sector = lax.axis_index("sector")
    sectors = lax.axis_size("sector")
    channels, rows, _ = left.shape
    cols = right.shape[2]
    cells = float(sectors * rows * sectors * cols)
    own = lax.dynamic_index_in_dim(pairs, sector, 0, keepdims=False).astype(F32)
    size = lax.dynamic_index_in_dim(left_sizes, sector, 0, keepdims=False)
    row = (jnp.arange(rows) < size).astype(F32)
    col = (jnp.arange(cols)[None, :] < right_sizes[:, None]).astype(F32) * own[:, None]
    valid = row[:, None] * col.reshape(1, -1)
    vector = wave * valid
    rights = lax.all_gather(right, "sector", axis=1)

    def image_of(v):
        half = jnp.einsum("wik,kbc->wibc", left, v.reshape(rows, sectors, cols), precision=EXACT)
        out = jnp.einsum("wibc,wbjc->ibj", half, rights, precision=EXACT)
        return lax.psum(out.reshape(rows, sectors * cols), "mpo") * valid

    first = image_of(vector)
    cross, square = lax.psum((jnp.sum(vector * first), jnp.sum(vector * vector)), "sector")
    value = cross / (square + TINY)
    residual = first - value * vector
    rest = lax.psum(jnp.sum(residual * residual), "sector")
    product = image_of(residual / jnp.sqrt(rest / cells + TINY))
    return product, jnp.reshape(value, (1,))


def solution(mesh):
    line = mesh.shape["sector"] == 4 and mesh.shape["mpo"] == 4
    return jax.shard_map(
        line_device if line else wide_device,
        mesh=mesh,
        in_specs=(
            P(("groups", "sector"), None),
            P("mpo", ("groups", "sector"), None),
            P("mpo", ("groups", "sector"), None),
            P("groups"),
            P("groups"),
            P("groups", None),
        ),
        out_specs=(P(("groups", "sector"), None), P("groups")),
        check_vma=False,
    )
```

```python
import functools

import jax
import jax.numpy as jnp
from jax import lax
from jax.experimental import pallas as pl
from jax.experimental.pallas import tpu as pltpu
from jax.sharding import PartitionSpec as P

EXACT = lax.Precision.HIGHEST
TINY = 1e-06
PARAMS = pltpu.CompilerParams(vmem_limit_bytes=32 * 1024 * 1024)
VMEM = pl.BlockSpec(memory_space=pltpu.VMEM)
SMEM = pl.BlockSpec(memory_space=pltpu.SMEM)
F32 = jnp.float32
BF16 = jnp.bfloat16

EARLY, LATE = (0, 1, 2), (3,)


def split(x):
    high = x.astype(BF16)
    rest = x - high.astype(F32)
    middle = rest.astype(BF16)
    return high, middle, (rest - middle.astype(F32)).astype(BF16)


def matmul(a, b, turned=False):
    return lax.dot_general(
        a, b, (((1,), (1 if turned else 0,)), ((), ())), preferred_element_type=F32
    )


def left_parts(a):
    high, middle, low = split(a)
    return jnp.concatenate([middle, high, low], axis=1)


def times(parts, x):
    depth, n = x.shape
    high, middle, low = split(x)
    large = jnp.concatenate([high, middle], axis=1)
    large = matmul(parts[:, : 2 * depth], jnp.concatenate([large, large], axis=0))
    small = matmul(parts[:, depth:], jnp.concatenate([low, high], axis=0))
    return (small + large[:, n:]) + large[:, :n]


def times_turned(a, b):
    m, n = a.shape[0], b.shape[0]
    a_high, a_middle, a_low = split(a)
    b_high, b_middle, b_low = split(b)
    large = matmul(
        jnp.concatenate([a_high, a_middle], axis=0),
        jnp.concatenate([b_high, b_middle], axis=0),
        turned=True,
    )
    small = matmul(
        jnp.concatenate([a_high, a_low], axis=1),
        jnp.concatenate([b_low, b_high], axis=1),
        turned=True,
    )
    return ((small + large[m:, n:]) + (large[m:, :n] + large[:m, n:])) + large[:m, :n]


def block_valid(left_sizes, right_sizes, pairs, a, b, rows, cols):
    row = lax.broadcasted_iota(jnp.int32, (rows, cols), 0) < left_sizes[a]
    col = lax.broadcasted_iota(jnp.int32, (rows, cols), 1) < right_sizes[b]
    return (row & col).astype(F32) * pairs[a, b].astype(F32)


def call(body, outs, n_small, n_big, flops=None):
    cost = None
    if flops is not None:
        cost = pl.CostEstimate(flops=flops, bytes_accessed=flops // 100, transcendentals=0)
    return pl.pallas_call(
        body,
        out_shape=outs,
        in_specs=[SMEM] * n_small + [VMEM] * n_big,
        out_specs=[VMEM] * len(outs),
        compiler_params=PARAMS,
        cost_estimate=cost,
    )


def slot_column(slot, sector):
    return sector ^ (0, 1, 3, 2)[slot]


def columns(b, width):
    return pl.ds(pl.multiple_of(b * width, width), width)


def channel_row(blocks):
    return jnp.concatenate([blocks[w] for w in range(blocks.shape[0])], axis=1)


def half_body(left_sizes, right_sizes, pairs, wave, left, right, vector, halfway, factors, valid, own):
    sector = lax.axis_index("sector")
    channels, rows, _ = left.shape
    slots, _, inner = halfway.shape
    cols = inner // channels
    factors[...] = left_parts(left[...].reshape(channels * rows, rows))
    for k in range(slots):
        b = slot_column(k, sector)
        valid[k] = block_valid(left_sizes, right_sizes, pairs, sector, b, rows, cols)
        vector[k] = wave[:, columns(b, cols)] * valid[k]
    part = times(factors[...], channel_row(vector))
    for k in range(slots):
        for w in range(channels):
            halfway[k, :, w * cols : (w + 1) * cols] = part[
                w * rows : (w + 1) * rows, k * cols : (k + 1) * cols
            ]
    own[0] = times_turned(halfway[0], channel_row(right))


def first_body(slots, halfway, *refs):
    out = refs[-1]
    for k, slot in enumerate(slots):
        out[k] = times_turned(halfway[slot], channel_row(refs[k]))


def ratio_of(cross, square):
    return jnp.where(square > 0, cross / jnp.where(square > 0, square, 1.0), 0.0)


def first_images(slots, own, other, valid, image):
    for k, slot in enumerate(slots):
        image[k] = (own[k] + other[k]) * valid[slot]


def second_images(factors, rights, image):
    slots, rows, cols = image.shape
    channels = factors.shape[0] // rows
    half = times(factors[...], channel_row(image))
    partials = []
    for k in range(slots):
        here = half[:, k * cols : (k + 1) * cols].reshape(channels, rows, cols)
        partials.append(times_turned(channel_row(here), channel_row(rights[k])))
    return partials


def write_sums(slots, vector, image, sums, at):
    cols = vector.shape[2]
    cross = jnp.zeros((1, cols), F32)
    square = jnp.zeros((1, cols), F32)
    for k, slot in enumerate(slots):
        v = vector[slot]
        cross += jnp.sum(v * image[k], axis=0, keepdims=True)
        square += jnp.sum(v * v, axis=0, keepdims=True)
    both = jnp.sum(jnp.concatenate([cross, square], axis=0), axis=1, keepdims=True)
    both = jnp.broadcast_to(both, (2, cols))
    ratio = ratio_of(both[0:1], both[1:2])
    rest = jnp.zeros((1, cols), F32)
    for k, slot in enumerate(slots):
        away = image[k] - ratio * vector[slot]
        rest += jnp.sum(away * away, axis=0, keepdims=True)
    sums[at : at + 2, :] = both
    sums[at + 2 : at + 3, :] = rest


def early_body(slots, own, other, valid, factors, vector, *refs):
    image, partial, sums = refs[-3:]
    first_images(slots, own, other, valid, image)
    sums[...] = jnp.zeros_like(sums)
    write_sums(slots, vector, image, sums, 0)
    for k, part in enumerate(second_images(factors, refs[:-3], image)):
        partial[k] = part


def late_body(early, slots, own, other, valid, factors, vector, sums_before, before, *refs):
    image, keep, send, sums = refs[-4:]
    first = lax.axis_index("mpo") % 2 == 0
    first_images(slots, own, other, valid, image)
    sums[...] = sums_before[...]
    write_sums(slots, vector, image, sums, 3)
    everything = {slot: before[k] for k, slot in enumerate(early)}
    everything.update(zip(slots, second_images(factors, refs[:-4], image)))
    for k in (0, 1):
        keep[k] = jnp.where(first, everything[k], everything[2 + k])
        send[k] = jnp.where(first, everything[2 + k], everything[k])


def scalar_body(groups, cells, near, far, scalars):
    def everyone(read):
        return (read(near, 0) + read(near, 8)) + (read(far, 0) + read(far, 8))

    def every_group(row):
        return lambda s, at: sum(s[at + row + 3 * g : at + row + 3 * g + 1, :] for g in range(groups))

    value = everyone(every_group(0)) / (everyone(every_group(1)) + TINY)

    def gaps(s, at):
        total = 0.0
        for row in range(at, at + 3 * groups, 3):
            square = s[row + 1 : row + 2, :]
            gap = ratio_of(s[row : row + 1, :], square) - value
            total += gap * (gap * square)
        return total

    rest = jnp.sum(everyone(every_group(2)), axis=1, keepdims=True) + everyone(gaps)
    scalars[0:1, :] = value
    scalars[1:2, :] = 1.0 / jnp.sqrt(rest / cells + TINY)


def last_body(groups, valid, scalars, total, others, *refs):
    product, ritz = refs[-2:]
    ritz[0] = scalars[0, 0]
    sector = lax.axis_index("sector")
    me = lax.axis_index("mpo") % 2
    cols = total.shape[2]
    value, scale = scalars[0:1, :], scalars[1:2, :]
    for slots, image in zip(groups, refs[:-2]):
        for k, slot in enumerate(slots):
            b = slot_column(slot, sector)
            second = jnp.where(me == slot // 2, total[slot % 2], others[slot % 2])
            product[:, columns(b, cols)] = (second * valid[slot] - value * image[k]) * scale


def line_device(wave, left, right, left_sizes, right_sizes, pairs):
    channels, rows, _ = left.shape
    cols = right.shape[2]
    sectors = 4
    cells = float(sectors * rows * sectors * cols)

    def near(x):
        return lax.ppermute(x, "sector", [(0, 1), (1, 0), (2, 3), (3, 2)])

    def far(x):
        return lax.ppermute(x, "sector", [(0, 2), (2, 0), (1, 3), (3, 1)])

    def mirror(x):
        return lax.ppermute(x, "sector", [(0, 3), (3, 0), (1, 2), (2, 1)])

    def core(x):
        return lax.ppermute(x, "mpo", [(0, 1), (1, 0), (2, 3), (3, 2)])

    def across(x):
        return lax.ppermute(x, "mpo", [(0, 2), (1, 3), (2, 0), (3, 1)])

    def shape(*dims, of=F32):
        return jax.ShapeDtypeStruct(dims, of)

    def after(x, *others):
        return lax.optimization_barrier((x, *others))[0]

    right_near = near(right)
    right_mirror = mirror(right)
    vector, halfway, factors, valid, own = call(
        half_body,
        [
            shape(sectors, rows, cols),
            shape(sectors, rows, channels * cols),
            shape(channels * rows, 3 * rows, of=BF16),
            shape(sectors, rows, cols),
            shape(1, rows, cols),
        ],
        3,
        3,
    )(left_sizes, right_sizes, pairs, wave, left, right)
    right_far = near(after(right_mirror, halfway))

    def partials(slots, halfway, *rights):
        return call(
            functools.partial(first_body, slots), [shape(len(slots), rows, cols)], 0, 1 + len(slots)
        )(halfway, *rights)[0]

    def chip_sum(x):
        return x + core(x)

    one = chip_sum(after(own, right_mirror))
    two = chip_sum(partials((1, 2), after(halfway, one), right_near, right_mirror))
    three = chip_sum(partials((3,), after(halfway, two), right_far))
    image_early, second_early, sums = call(
        functools.partial(early_body, EARLY),
        [shape(3, rows, cols), shape(3, rows, cols), shape(8, cols)],
        0,
        8,
    )(
        jnp.concatenate([one, two]),
        jnp.concatenate([across(one), across(two)]),
        valid,
        factors,
        vector,
        right,
        right_near,
        right_mirror,
    )
    image_late, keep, send, sums = call(
        functools.partial(late_body, EARLY, LATE),
        [shape(1, rows, cols), shape(2, rows, cols), shape(2, rows, cols), shape(8, cols)],
        0,
        8,
    )(three, across(three), valid, factors, vector, sums, second_early, right_far)

    mine = keep + core(send)
    sums_near = jnp.concatenate([sums, near(sums)])
    sums_far = far(sums_near)
    total = mine + across(mine)
    others = core(total)
    (scalars,) = call(
        functools.partial(scalar_body, 2, cells), [shape(8, cols)], 0, 2, flops=3_000_000_000
    )(sums_near, sums_far)
    product, ritz = pl.pallas_call(
        functools.partial(last_body, (EARLY, LATE)),
        out_shape=[shape(rows, sectors * cols), shape(1)],
        in_specs=[VMEM] * 6,
        out_specs=[VMEM, SMEM],
        compiler_params=PARAMS,
    )(valid, scalars, total, others, image_early, image_late)
    return product, ritz


def wide_device(wave, left, right, left_sizes, right_sizes, pairs):
    sector = lax.axis_index("sector")
    sectors = lax.axis_size("sector")
    channels, rows, _ = left.shape
    cols = right.shape[2]
    cells = float(sectors * rows * sectors * cols)
    own = lax.dynamic_index_in_dim(pairs, sector, 0, keepdims=False).astype(F32)
    size = lax.dynamic_index_in_dim(left_sizes, sector, 0, keepdims=False)
    row = (jnp.arange(rows) < size).astype(F32)
    col = (jnp.arange(cols)[None, :] < right_sizes[:, None]).astype(F32) * own[:, None]
    valid = row[:, None] * col.reshape(1, -1)
    vector = wave * valid
    rights = lax.all_gather(right, "sector", axis=1)

    def image_of(v):
        half = jnp.einsum("wik,kbc->wibc", left, v.reshape(rows, sectors, cols), precision=EXACT)
        out = jnp.einsum("wibc,wbjc->ibj", half, rights, precision=EXACT)
        return lax.psum(out.reshape(rows, sectors * cols), "mpo") * valid

    first = image_of(vector)
    cross, square = lax.psum((jnp.sum(vector * first), jnp.sum(vector * vector)), "sector")
    value = cross / (square + TINY)
    residual = first - value * vector
    rest = lax.psum(jnp.sum(residual * residual), "sector")
    product = image_of(residual / jnp.sqrt(rest / cells + TINY))
    return product, jnp.reshape(value, (1,))


def solution(mesh):
    line = mesh.shape["sector"] == 4 and mesh.shape["mpo"] == 4
    return jax.shard_map(
        line_device if line else wide_device,
        mesh=mesh,
        in_specs=(
            P(("groups", "sector"), None),
            P("mpo", ("groups", "sector"), None),
            P("mpo", ("groups", "sector"), None),
            P("groups"),
            P("groups"),
            P("groups", None),
        ),
        out_specs=(P(("groups", "sector"), None), P("groups")),
        check_vma=False,
    )
```

```python
import functools

import jax
import jax.numpy as jnp
from jax import lax
from jax.experimental import pallas as pl
from jax.experimental.pallas import tpu as pltpu
from jax.sharding import PartitionSpec as P

EXACT = lax.Precision.HIGHEST
TINY = 1e-06
PARAMS = pltpu.CompilerParams(vmem_limit_bytes=32 * 1024 * 1024)
VMEM = pl.BlockSpec(memory_space=pltpu.VMEM)
SMEM = pl.BlockSpec(memory_space=pltpu.SMEM)
F32 = jnp.float32
BF16 = jnp.bfloat16

EARLY, LATE = (0, 1, 2), (3,)


def split(x):
    high = x.astype(BF16)
    rest = x - high.astype(F32)
    middle = rest.astype(BF16)
    return high, middle, (rest - middle.astype(F32)).astype(BF16)


def matmul(a, b, turned=False):
    return lax.dot_general(
        a, b, (((1,), (1 if turned else 0,)), ((), ())), preferred_element_type=F32
    )


def left_parts(a):
    high, middle, low = split(a)
    return jnp.concatenate([middle, high, low], axis=1)


def times(parts, x):
    depth, n = x.shape
    high, middle, low = split(x)
    large = jnp.concatenate([high, middle], axis=1)
    large = matmul(parts[:, : 2 * depth], jnp.concatenate([large, large], axis=0))
    small = matmul(parts[:, depth:], jnp.concatenate([low, high], axis=0))
    return (small + large[:, n:]) + large[:, :n]


def times_turned(a, b):
    m, n = a.shape[0], b.shape[0]
    a_high, a_middle, a_low = split(a)
    b_high, b_middle, b_low = split(b)
    large = matmul(
        jnp.concatenate([a_high, a_middle], axis=0),
        jnp.concatenate([b_high, b_middle], axis=0),
        turned=True,
    )
    small = matmul(
        jnp.concatenate([a_high, a_low], axis=1),
        jnp.concatenate([b_low, b_high], axis=1),
        turned=True,
    )
    return ((small + large[m:, n:]) + (large[m:, :n] + large[:m, n:])) + large[:m, :n]


def block_valid(left_sizes, right_sizes, pairs, a, b, rows, cols):
    row = lax.broadcasted_iota(jnp.int32, (rows, cols), 0) < left_sizes[a]
    col = lax.broadcasted_iota(jnp.int32, (rows, cols), 1) < right_sizes[b]
    return (row & col).astype(F32) * pairs[a, b].astype(F32)


def call(body, outs, n_small, n_big, flops=None):
    cost = None
    if flops is not None:
        cost = pl.CostEstimate(flops=flops, bytes_accessed=flops // 100, transcendentals=0)
    return pl.pallas_call(
        body,
        out_shape=outs,
        in_specs=[SMEM] * n_small + [VMEM] * n_big,
        out_specs=[VMEM] * len(outs),
        compiler_params=PARAMS,
        cost_estimate=cost,
    )


def slot_column(slot, sector):
    return sector ^ (0, 1, 3, 2)[slot]


def columns(b, width):
    return pl.ds(pl.multiple_of(b * width, width), width)


def channel_row(blocks):
    return jnp.concatenate([blocks[w] for w in range(blocks.shape[0])], axis=1)


def half_body(left_sizes, right_sizes, pairs, wave, left, vector, halfway, factors, valid):
    sector = lax.axis_index("sector")
    channels, rows, _ = left.shape
    slots, _, inner = halfway.shape
    cols = inner // channels
    factors[...] = left_parts(left[...].reshape(channels * rows, rows))
    for k in range(slots):
        b = slot_column(k, sector)
        valid[k] = block_valid(left_sizes, right_sizes, pairs, sector, b, rows, cols)
        vector[k] = wave[:, columns(b, cols)] * valid[k]
    part = times(factors[...], channel_row(vector))
    for k in range(slots):
        for w in range(channels):
            halfway[k, :, w * cols : (w + 1) * cols] = part[
                w * rows : (w + 1) * rows, k * cols : (k + 1) * cols
            ]


def first_body(slots, halfway, *refs):
    out = refs[-1]
    for k, slot in enumerate(slots):
        out[k] = times_turned(halfway[slot], channel_row(refs[k]))


def ratio_of(cross, square):
    return jnp.where(square > 0, cross / jnp.where(square > 0, square, 1.0), 0.0)


def first_images(slots, own, other, valid, image):
    for k, slot in enumerate(slots):
        image[k] = (own[k] + other[k]) * valid[slot]


def second_images(factors, rights, image):
    slots, rows, cols = image.shape
    channels = factors.shape[0] // rows
    half = times(factors[...], channel_row(image))
    partials = []
    for k in range(slots):
        here = half[:, k * cols : (k + 1) * cols].reshape(channels, rows, cols)
        partials.append(times_turned(channel_row(here), channel_row(rights[k])))
    return partials


def write_sums(slots, vector, image, sums, at):
    cols = vector.shape[2]
    cross = jnp.zeros((1, cols), F32)
    square = jnp.zeros((1, cols), F32)
    for k, slot in enumerate(slots):
        v = vector[slot]
        cross += jnp.sum(v * image[k], axis=0, keepdims=True)
        square += jnp.sum(v * v, axis=0, keepdims=True)
    both = jnp.sum(jnp.concatenate([cross, square], axis=0), axis=1, keepdims=True)
    both = jnp.broadcast_to(both, (2, cols))
    ratio = ratio_of(both[0:1], both[1:2])
    rest = jnp.zeros((1, cols), F32)
    for k, slot in enumerate(slots):
        away = image[k] - ratio * vector[slot]
        rest += jnp.sum(away * away, axis=0, keepdims=True)
    sums[at : at + 2, :] = both
    sums[at + 2 : at + 3, :] = rest


def early_body(slots, own, other, valid, factors, vector, *refs):
    image, partial, sums = refs[-3:]
    first_images(slots, own, other, valid, image)
    sums[...] = jnp.zeros_like(sums)
    write_sums(slots, vector, image, sums, 0)
    for k, part in enumerate(second_images(factors, refs[:-3], image)):
        partial[k] = part


def late_body(early, slots, own, other, valid, factors, vector, sums_before, before, *refs):
    image, keep, send, sums = refs[-4:]
    first = lax.axis_index("mpo") % 2 == 0
    first_images(slots, own, other, valid, image)
    sums[...] = sums_before[...]
    write_sums(slots, vector, image, sums, 3)
    everything = {slot: before[k] for k, slot in enumerate(early)}
    everything.update(zip(slots, second_images(factors, refs[:-4], image)))
    for k in (0, 1):
        keep[k] = jnp.where(first, everything[k], everything[2 + k])
        send[k] = jnp.where(first, everything[2 + k], everything[k])


def scalar_body(groups, cells, near, far, valid, total, early, late, scalars, done):
    def everyone(read):
        return (read(near, 0) + read(near, 8)) + (read(far, 0) + read(far, 8))

    def every_group(row):
        return lambda s, at: sum(s[at + row + 3 * g : at + row + 3 * g + 1, :] for g in range(groups))

    value = everyone(every_group(0)) / (everyone(every_group(1)) + TINY)

    def gaps(s, at):
        total = 0.0
        for row in range(at, at + 3 * groups, 3):
            square = s[row + 1 : row + 2, :]
            gap = ratio_of(s[row : row + 1, :], square) - value
            total += gap * (gap * square)
        return total

    rest = jnp.sum(everyone(every_group(2)), axis=1, keepdims=True) + everyone(gaps)
    scalars[0:1, :] = value
    scale = 1.0 / jnp.sqrt(rest / cells + TINY)
    scalars[1:2, :] = scale
    me = lax.axis_index("mpo") % 2
    for k, image in enumerate((early[2], late[0])):
        image = jnp.where(me == 0, early[k], image)
        done[k] = (total[k] * valid[2 * me + k] - value * image) * scale


def last_body(groups, valid, scalars, total, others, *refs):
    product, ritz = refs[-2:]
    ritz[0] = scalars[0, 0]
    sector = lax.axis_index("sector")
    me = lax.axis_index("mpo") % 2
    cols = total.shape[2]
    value, scale = scalars[0:1, :], scalars[1:2, :]
    for slots, image in zip(groups, refs[:-2]):
        for k, slot in enumerate(slots):
            b = slot_column(slot, sector)
            other = (others[slot % 2] * valid[slot] - value * image[k]) * scale
            product[:, columns(b, cols)] = jnp.where(me == slot // 2, total[slot % 2], other)


def line_device(wave, left, right, left_sizes, right_sizes, pairs):
    channels, rows, _ = left.shape
    cols = right.shape[2]
    sectors = 4
    cells = float(sectors * rows * sectors * cols)

    def near(x):
        return lax.ppermute(x, "sector", [(0, 1), (1, 0), (2, 3), (3, 2)])

    def far(x):
        return lax.ppermute(x, "sector", [(0, 2), (2, 0), (1, 3), (3, 1)])

    def mirror(x):
        return lax.ppermute(x, "sector", [(0, 3), (3, 0), (1, 2), (2, 1)])

    def core(x):
        return lax.ppermute(x, "mpo", [(0, 1), (1, 0), (2, 3), (3, 2)])

    def across(x):
        return lax.ppermute(x, "mpo", [(0, 2), (1, 3), (2, 0), (3, 1)])

    def shape(*dims, of=F32):
        return jax.ShapeDtypeStruct(dims, of)

    def after(x, *others):
        return lax.optimization_barrier((x, *others))[0]

    right_near = near(right)
    right_mirror = mirror(right)
    vector, halfway, factors, valid = call(
        half_body,
        [
            shape(sectors, rows, cols),
            shape(sectors, rows, channels * cols),
            shape(channels * rows, 3 * rows, of=BF16),
            shape(sectors, rows, cols),
        ],
        3,
        2,
    )(left_sizes, right_sizes, pairs, wave, left)
    right_far = near(after(right_mirror, halfway))

    def partials(slots, halfway, *rights):
        return call(
            functools.partial(first_body, slots), [shape(len(slots), rows, cols)], 0, 1 + len(slots)
        )(halfway, *rights)[0]

    def chip_sum(x):
        return x + core(x)

    one = chip_sum(after(partials((0,), halfway, right), right_mirror))
    two = chip_sum(partials((1, 2), after(halfway, one), right_near, right_mirror))
    three = chip_sum(partials((3,), after(halfway, two), right_far))
    image_early, second_early, sums = call(
        functools.partial(early_body, EARLY),
        [shape(3, rows, cols), shape(3, rows, cols), shape(8, cols)],
        0,
        8,
    )(
        jnp.concatenate([one, two]),
        jnp.concatenate([across(one), across(two)]),
        valid,
        factors,
        vector,
        right,
        right_near,
        right_mirror,
    )
    image_late, keep, send, sums = call(
        functools.partial(late_body, EARLY, LATE),
        [shape(1, rows, cols), shape(2, rows, cols), shape(2, rows, cols), shape(8, cols)],
        0,
        8,
    )(three, across(three), valid, factors, vector, sums, second_early, right_far)

    mine = keep + core(send)
    sums_near = jnp.concatenate([sums, near(sums)])
    sums_far = far(sums_near)
    total = mine + across(mine)
    others = core(total)
    scalars, done = call(
        functools.partial(scalar_body, 2, cells),
        [shape(8, cols), shape(2, rows, cols)],
        0,
        6,
        flops=3_000_000_000,
    )(sums_near, sums_far, valid, total, image_early, image_late)
    product, ritz = pl.pallas_call(
        functools.partial(last_body, (EARLY, LATE)),
        out_shape=[shape(rows, sectors * cols), shape(1)],
        in_specs=[VMEM] * 6,
        out_specs=[VMEM, SMEM],
        compiler_params=PARAMS,
    )(valid, scalars, done, others, image_early, image_late)
    return product, ritz


def wide_device(wave, left, right, left_sizes, right_sizes, pairs):
    sector = lax.axis_index("sector")
    sectors = lax.axis_size("sector")
    channels, rows, _ = left.shape
    cols = right.shape[2]
    cells = float(sectors * rows * sectors * cols)
    own = lax.dynamic_index_in_dim(pairs, sector, 0, keepdims=False).astype(F32)
    size = lax.dynamic_index_in_dim(left_sizes, sector, 0, keepdims=False)
    row = (jnp.arange(rows) < size).astype(F32)
    col = (jnp.arange(cols)[None, :] < right_sizes[:, None]).astype(F32) * own[:, None]
    valid = row[:, None] * col.reshape(1, -1)
    vector = wave * valid
    rights = lax.all_gather(right, "sector", axis=1)

    def image_of(v):
        half = jnp.einsum("wik,kbc->wibc", left, v.reshape(rows, sectors, cols), precision=EXACT)
        out = jnp.einsum("wibc,wbjc->ibj", half, rights, precision=EXACT)
        return lax.psum(out.reshape(rows, sectors * cols), "mpo") * valid

    first = image_of(vector)
    cross, square = lax.psum((jnp.sum(vector * first), jnp.sum(vector * vector)), "sector")
    value = cross / (square + TINY)
    residual = first - value * vector
    rest = lax.psum(jnp.sum(residual * residual), "sector")
    product = image_of(residual / jnp.sqrt(rest / cells + TINY))
    return product, jnp.reshape(value, (1,))


def solution(mesh):
    line = mesh.shape["sector"] == 4 and mesh.shape["mpo"] == 4
    return jax.shard_map(
        line_device if line else wide_device,
        mesh=mesh,
        in_specs=(
            P(("groups", "sector"), None),
            P("mpo", ("groups", "sector"), None),
            P("mpo", ("groups", "sector"), None),
            P("groups"),
            P("groups"),
            P("groups", None),
        ),
        out_specs=(P(("groups", "sector"), None), P("groups")),
        check_vma=False,
    )
```
